256 devices in a mesh: row: 64 (over y, z_hi, x), col: 4 (over z_lo, core).
Axes of the slice: x: 4, y: 4, z: 8 (z_hi: 4, z_lo: 2; z = z_hi * 2 + z_lo), core: 2. Of those that a mesh axis runs over, the one named last changes fastest.
Arguments:
- cotangent: bfloat16 [1024, 28672], P('col', 'row'), may hold values from -0.1875 to 0.1875
- activations: bfloat16 [1024, 8192], P('col', 'row'), may hold values from -6 to 6
- shard_of_token: int32 [1024], P('col'), may hold values from 0 to 2047
- shard_weight: float32 [2048], replicated, may hold values from 0.25 to 4
- hidden_basis: bfloat16 [28672, 28672], P('row', 'col'), may hold values from -0.03125 to 0.03125
- input_basis: bfloat16 [8192, 8192], P('col', 'row'), may hold values from -0.0625 to 0.0625
- eigenvalues: bfloat16 [28672, 8192], P('col', 'row'), may hold values from 0.099609375 to 2
- panel_order: int32 [2], replicated, may hold values from 0 to 111, as said below
Outputs:
- influence_direction: bfloat16 [28672, 8192], P('row', 'col')
The draws below stay inside these ranges and needn't reach their ends.
Inputs may be any that keep to these rules, and one draw needn't show every extreme that they name: `panel_order`: the 2 panels of the window are all different, and the last panel, number 28672 / 256 - 1, is always one of them.
All inputs are finite; a program needn't handle non-finite values.
Results may differ from the reference program's by a relative error of at most 0.025.
Values may be sent and summed in bfloat16 or wider, within the bound.
A program may use at most 128 MiB of HBM per device.

```python
import math
import jax
import jax.numpy as jnp
from jax import lax

D = 8192
FF = 28672
SHARDS = 2048
PANEL = 256
STEPS = 2
TOKENS = 1024


def draw_panel_order(key, part):
    key = jax.random.fold_in(key, 11)
    pick_key = jax.random.fold_in(key, 1)
    place_key = jax.random.fold_in(key, 2)
    last_panel = FF // PANEL - 1
    others = jax.random.permutation(pick_key, last_panel)[:STEPS - 1].astype(jnp.int32)
    joined = jnp.concatenate([others, jnp.full((1,), last_panel, jnp.int32)])
    place = jax.random.randint(place_key, (), 0, STEPS).astype(jnp.int32)
    index = jnp.arange(STEPS, dtype=jnp.int32)
    moved = jnp.where(index == place, STEPS - 1, jnp.where(index == STEPS - 1, place, index))
    return joined[moved].astype(jnp.int32)


def place_ends(result, stream_key, smallest, high):
    longest = result.shape.index(max(result.shape))
    spots = []
    for shift in (0, 1):
        where = [jax.random.randint(jax.random.fold_in(stream_key, axis), (), 0, length) for axis, length in enumerate(result.shape)]
        where[longest] = (where[longest] + shift) % result.shape[longest]
        spots.append(tuple(where))
    return result.at[spots[0]].set(smallest).at[spots[1]].set(high)


def block_levels(own_key, extent, pieces, least, high):
    def one(axis_at, parts):
        steps = jax.random.uniform(jax.random.fold_in(jax.random.fold_in(own_key, 6), axis_at), (parts,), jnp.float32, least / len(pieces), high / len(pieces))
        return jnp.repeat(jnp.exp(steps), extent[axis_at] // parts).reshape((-1,) + (1,) * (len(extent) - axis_at - 1))

    gain = one(*pieces[0])
    for cut in pieces[1:]:
        gain = gain * one(*cut)
    return gain


def gaussian(key, dims, deviation, most, cuts=(), kind=jnp.bfloat16):
    result = jax.random.normal(key, dims, jnp.float32) * deviation
    if len(cuts) > 0:
        result = block_levels(key, dims, cuts, -0.22, 0.18) * result
    return jnp.clip(result, min=-most, max=most).astype(kind)


def setup_inputs(seed: int = 0) -> dict:
    key_list = jax.random.split(jax.random.key(seed), 9)
    return {
        "cotangent": gaussian(key_list[0], (TOKENS, FF), TOKENS ** -0.5, 0.1875, ((0, 4), (1, 64))),
        "activations": gaussian(key_list[1], (TOKENS, D), 1.0, 6.0, ((0, 4), (1, 64))),
        "shard_of_token": place_ends(jax.random.randint(key_list[2], (TOKENS,), 0, SHARDS), jax.random.fold_in(key_list[2], 1), 0, SHARDS - 1).astype(jnp.int32),
        "shard_weight": jnp.clip(jnp.exp(jax.random.uniform(key_list[3], (SHARDS,), jnp.float32, math.log(0.25), math.log(4.0))), 0.25, 4.0),
        "hidden_basis": gaussian(key_list[4], (FF, FF), FF ** -0.5, 0.03125, ((0, 64), (1, 4))),
        "input_basis": gaussian(key_list[5], (D, D), D ** -0.5, 0.0625, ((0, 4), (1, 64))),
        "eigenvalues": jnp.clip(jnp.exp(math.log(2.0) - 2.9996462 * jax.random.uniform(key_list[6], (FF, D), jnp.float32) ** block_levels(key_list[6], (FF, D), ((0, 4), (1, 64)), -0.2, 0.2)), 0.099609375, 2.0).astype(jnp.bfloat16),
        "panel_order": draw_panel_order(jax.random.fold_in(key_list[8], 71), 0),
    }


DAMPING = 0.01


def reference(cotangent, activations, shard_of_token, shard_weight, hidden_basis, input_basis, eigenvalues, panel_order):
    token_weight = shard_weight[shard_of_token]
    scaled = (cotangent.astype(jnp.float32) * token_weight[:, None]).astype(jnp.bfloat16)
    basis_parts = []
    eigen_parts = []
    for step in range(STEPS):
        start = (panel_order[step] * PANEL).astype(jnp.int32)
        basis_parts.append(lax.dynamic_slice_in_dim(hidden_basis, start, PANEL, 1))
        eigen_parts.append(lax.dynamic_slice_in_dim(eigenvalues, start, PANEL, 0))
    basis_window = jnp.concatenate(basis_parts, axis=1)
    eigen_window = jnp.concatenate(eigen_parts, axis=0)
    projected = lax.dot_general(basis_window, scaled, (((0,), (1,)), ((), ())), preferred_element_type=jnp.float32)
    rotated = jnp.dot(projected, activations.astype(jnp.float32), precision=lax.Precision.HIGHEST).astype(jnp.bfloat16)
    turned = jnp.dot(rotated, input_basis, preferred_element_type=jnp.float32)
    coefficients = (turned / (eigen_window.astype(jnp.float32) + DAMPING)).astype(jnp.bfloat16)
    returned = lax.dot_general(coefficients, input_basis, (((1,), (1,)), ((), ())), preferred_element_type=jnp.float32).astype(jnp.bfloat16)
    return jnp.dot(basis_window, returned, preferred_element_type=jnp.float32).astype(jnp.bfloat16)
```

```python
import jax
import jax.numpy as jnp
from jax import lax
from jax.experimental import pallas as pl
from jax.experimental.pallas import tpu as pltpu
from jax.sharding import PartitionSpec as P

PANEL = 256
LAST = 111
PER_COL = 28
DAMPING = 0.01
MESH = pl.DeviceIdType.MESH
F32 = jnp.float32
BF16 = jnp.bfloat16

(S_ACT, S_BAS, S_EIX, S_EIC, S_H, S_PX, S_PY, S_PZ, S_PG, S_RC, S_RZ, S_RY, S_TC, S_CC, S_QY, S_QZ,
 S_GZ, S_GY0, S_GX0, S_GX1, S_GY1, N_STAGES) = range(22)


def pick(order_hbm, hid_hbm, eig_hbm, h_src, e_src, order, sems):
    col = lax.axis_index("col")
    cp = pltpu.make_async_copy(order_hbm, order, sems.at[0])
    cp.start()
    cp.wait()
    other = order[0] + order[1] - LAST
    place = pl.multiple_of((other - col * PER_COL) * PANEL, PANEL)
    mine = (other >= col * PER_COL) & (other < (col + 1) * PER_COL)
    end = (PER_COL - 1) * PANEL

    def fetch(have, at, k):
        h_part = h_src.at[:, PANEL * k:PANEL * (k + 1)]
        e_part = e_src.at[PANEL * k:PANEL * (k + 1)]

        def copies():
            return (pltpu.make_async_copy(hid_hbm.at[:, pl.ds(at, PANEL)], h_part, sems.at[1 + 2 * k]),
                    pltpu.make_async_copy(eig_hbm.at[pl.ds(at, PANEL)], e_part, sems.at[2 + 2 * k]))

        @pl.when(have)
        def _():
            for cp in copies():
                cp.start()

        @pl.when(jnp.logical_not(have))
        def _():
            h_part[...] = jnp.zeros(h_part.shape, BF16)
            e_part[...] = jnp.zeros(e_part.shape, BF16)

        @pl.when(have)
        def _():
            for cp in copies():
                cp.wait()

    fetch(mine, place, 0)
    fetch(col == 3, end, 1)


def kernel(
    cot_hbm, act_hbm, shard_hbm, weight_hbm, bas_hbm, h_src, e_src, out_hbm,
    cot_t, cot, shard_ref, weight_ref, act_g, bas_g,
    e_x, e_c,
    h_a, h_b, h_win,
    p_src, p_x, p_y0, p_y, p_z0, p_z, p_g,
    r_src, r_c, r_full,
    t_src, t_c, c_all,
    q_src, q_y, q_z0, q_z, ret,
    out_buf,
    ssem, rsem, lsem, osem,
):
    row = lax.axis_index("row")
    col = lax.axis_index("col")
    x = row % 4
    zh = (row // 4) % 4
    y = row // 16
    core = col % 2

    def at_x(j):
        return (y * 16 + zh * 4 + j, col)

    def at_y(j):
        return (j * 16 + zh * 4 + x, col)

    def at_z(j):
        return (y * 16 + j * 4 + x, col)

    def at_c(j):
        return (row, j)

    sends = []

    def send(stage, slot, src, dst, sem_at, device):
        cp = pltpu.make_async_remote_copy(
            src_ref=src, dst_ref=dst, send_sem=ssem.at[stage, slot], recv_sem=rsem.at[stage, sem_at],
            device_id=device, device_id_type=MESH)
        cp.start()
        sends.append(cp)

    def arrived(stage, sem_at, dst, device):
        pltpu.make_async_remote_copy(
            src_ref=dst, dst_ref=dst, send_sem=ssem.at[stage, 0], recv_sem=rsem.at[stage, sem_at],
            device_id=device, device_id_type=MESH).wait_recv()

    def start(stage, me, place, src_of, dst):
        for d in (2, 1, 3):
            j = (me + d) % 4
            send(stage, d, src_of(j), dst, me, place(j))

    def finish(stage, me, place, dst_of):
        for d in (1, 3, 2):
            j = (me + d) % 4
            arrived(stage, j, dst_of(j), place(j))

    loads = [
        pltpu.make_async_copy(shard_hbm, shard_ref, lsem.at[0]),
        pltpu.make_async_copy(weight_hbm, weight_ref, lsem.at[1]),
        pltpu.make_async_copy(cot_hbm, cot_t, lsem.at[2]),
        pltpu.make_async_copy(act_hbm, act_g.at[x], lsem.at[3]),
        pltpu.make_async_copy(bas_hbm, bas_g.at[x], lsem.at[4]),
    ]
    for cp in loads:
        cp.start()

    barrier = pltpu.get_barrier_semaphore()
    for me, place in ((x, at_x), (y, at_y), (zh, at_z), (col, at_c)):
        for d in (1, 2, 3):
            pl.semaphore_signal(barrier, inc=1, device_id=place((me + d) % 4), device_id_type=MESH)

    pl.semaphore_wait(barrier, 12)

    keep = pl.multiple_of(core * 224, 224)
    give = pl.multiple_of((1 - core) * 224, 224)
    sibling = at_c(col + 1 - 2 * core)
    partner = at_c((col + 2) % 4)
    send(S_H, 0, h_src.at[pl.ds(give, 224)], h_a, 0, sibling)
    start(S_ACT, x, at_x, lambda j: act_hbm, act_g.at[x])

    loads[0].wait()
    loads[1].wait()
    ids = jnp.transpose(jnp.broadcast_to(shard_ref[...].astype(F32), (128, 256)))
    lane = lax.broadcasted_iota(jnp.int32, (256, 128), 1).astype(F32)
    weight = jnp.zeros((256, 128), F32)
    for j in range(16):
        weight = weight + jnp.where(ids == lane + float(128 * j), weight_ref[j:j + 1, :], 0.0)
    weight = jnp.sum(weight, axis=1, keepdims=True)

    arrived(S_H, 0, h_a, sibling)
    h_a[...] = h_a[...] + h_src[pl.ds(keep, 224)]
    send(S_H, 1, h_a, h_b, 1, partner)
    loads[2].wait()
    cot[...] = (jnp.transpose(cot_t[...].astype(F32)) * weight).astype(BF16)
    arrived(S_H, 1, h_b, partner)
    h_win[pl.ds(keep, 224)] = h_a[...] + h_b[...]
    send(S_H, 2, h_win.at[pl.ds(keep, 224)], h_win.at[pl.ds(keep, 224)], 2, sibling)
    arrived(S_H, 2, h_win.at[pl.ds(give, 224)], sibling)

    for j in range(4):
        p_src[j] = jnp.dot(cot[...], h_win[:, 128 * j:128 * (j + 1)], preferred_element_type=F32).astype(BF16)
    start(S_PX, x, at_x, lambda j: p_src.at[j], p_x.at[x])

    e_x[x] = e_src[pl.ds(pl.multiple_of(128 * x, 128), 128)]
    start(S_EIX, x, at_x, lambda j: e_src.at[pl.ds(pl.multiple_of(128 * j, 128), 128)], e_x.at[x])

    finish(S_PX, x, at_x, lambda j: p_x.at[j])
    p_x[x] = p_src[x]
    start(S_BAS, x, at_x, lambda j: bas_hbm, bas_g.at[x])
    total = (p_x[0].astype(F32) + p_x[1].astype(F32)) + (p_x[2].astype(F32) + p_x[3].astype(F32))
    for j in range(4):
        p_y0[j] = total[64 * j:64 * (j + 1)].astype(BF16)
    start(S_PY, y, at_y, lambda j: p_y0.at[j], p_y.at[y])
    p_y[y] = p_y0[y]
    finish(S_PY, y, at_y, lambda j: p_y.at[j])
    p_z0[...] = ((p_y[0].astype(F32) + p_y[1].astype(F32)) + (p_y[2].astype(F32) + p_y[3].astype(F32))).astype(BF16)
    start(S_PZ, zh, at_z, lambda j: p_z0, p_z.at[zh])
    p_z[zh] = p_z0[...]
    finish(S_EIX, x, at_x, lambda j: e_x.at[j])
    start(S_EIC, col, at_c, lambda j: e_x.at[j], e_c.at[col])
    e_c[col] = e_x[col]
    finish(S_PZ, zh, at_z, lambda j: p_z.at[j])
    p_g[y] = ((p_z[0].astype(F32) + p_z[1].astype(F32)) + (p_z[2].astype(F32) + p_z[3].astype(F32))).astype(BF16)
    start(S_PG, y, at_y, lambda j: p_g.at[y], p_g.at[y])
    loads[3].wait()
    finish(S_ACT, x, at_x, lambda j: act_g.at[j])
    finish(S_PG, y, at_y, lambda j: p_g.at[j])

    pk = jnp.transpose(p_g[...].reshape(256, 128).astype(F32)).astype(BF16)
    for j in range(4):
        r_src[:, 128 * j:128 * (j + 1)] = jnp.dot(pk, act_g[j], preferred_element_type=F32).astype(BF16)

    diagonal = col == y

    @pl.when(jnp.logical_not(diagonal))
    def _():
        cp = pltpu.make_async_remote_copy(
            src_ref=r_src, dst_ref=r_c.at[col], send_sem=ssem.at[S_RC, 0], recv_sem=rsem.at[S_RC, col],
            device_id=at_c(y), device_id_type=MESH)
        cp.start()
        cp.wait_send()

    @pl.when(diagonal)
    def _():
        r_c[col] = r_src[...]
        finish(S_RC, col, at_c, lambda j: r_c.at[j])
        r_full[zh] = ((r_c[0].astype(F32) + r_c[1].astype(F32)) + (r_c[2].astype(F32) + r_c[3].astype(F32))).astype(BF16)
        cps = []
        for d in (2, 1, 3):
            j = (zh + d) % 4
            cp = pltpu.make_async_remote_copy(
                src_ref=r_full.at[zh], dst_ref=r_full.at[zh], send_sem=ssem.at[S_RZ, d], recv_sem=rsem.at[S_RZ, zh],
                device_id=at_z(j), device_id_type=MESH)
            cp.start()
            cps.append(cp)
        finish(S_RZ, zh, at_z, lambda j: r_full.at[j])
        for d in (2, 1, 3):
            j = (y + d) % 4
            cp = pltpu.make_async_remote_copy(
                src_ref=r_full, dst_ref=r_full, send_sem=ssem.at[S_RY, d], recv_sem=rsem.at[S_RY, 0],
                device_id=at_y(j), device_id_type=MESH)
            cp.start()
            cps.append(cp)
        for cp in cps:
            cp.wait_send()

    @pl.when(jnp.logical_not(diagonal))
    def _():
        arrived(S_RY, 0, r_full, at_y(col))

    loads[4].wait()
    finish(S_BAS, x, at_x, lambda j: bas_g.at[j])
    for j in range(4):
        acc = jnp.dot(r_full[0], bas_g[j, 0:512], preferred_element_type=F32)
        for z in range(1, 4):
            acc = acc + jnp.dot(r_full[z], bas_g[j, 512 * z:512 * (z + 1)], preferred_element_type=F32)
        t_src[j] = acc.astype(BF16)
    start(S_TC, col, at_c, lambda j: t_src.at[j], t_c.at[col])
    t_c[col] = t_src[col]
    finish(S_EIC, col, at_c, lambda j: e_c.at[j])
    damped = (e_c[0].astype(F32) + e_c[1].astype(F32)) + (e_c[2].astype(F32) + e_c[3].astype(F32)) + DAMPING
    finish(S_TC, col, at_c, lambda j: t_c.at[j])
    turned = (t_c[0].astype(F32) + t_c[1].astype(F32)) + (t_c[2].astype(F32) + t_c[3].astype(F32))
    c_all[col] = (turned / damped).astype(BF16)
    start(S_CC, col, at_c, lambda j: c_all.at[col], c_all.at[col])
    finish(S_CC, col, at_c, lambda j: c_all.at[j])

    for z in range(4):
        acc = None
        for j in range(4):
            term = lax.dot_general(
                c_all[j], bas_g[j, 512 * z:512 * (z + 1)], (((1,), (1,)), ((), ())), preferred_element_type=F32)
            acc = term if acc is None else acc + term
        acc = acc.astype(BF16)
        for j in range(4):
            q_src[j, z] = acc[32 * j:32 * (j + 1)]
    start(S_QY, y, at_y, lambda j: q_src.at[j], q_y.at[y])
    q_y[y] = q_src[y]
    finish(S_QY, y, at_y, lambda j: q_y.at[j])
    for z in range(4):
        q_z0[z] = ((q_y[0, z].astype(F32) + q_y[1, z].astype(F32)) + (q_y[2, z].astype(F32) + q_y[3, z].astype(F32))).astype(BF16)
    start(S_QZ, zh, at_z, lambda j: q_z0.at[j], q_z.at[zh])
    q_z[zh] = q_z0[zh]
    finish(S_QZ, zh, at_z, lambda j: q_z.at[j])
    piece = ((q_z[0].astype(F32) + q_z[1].astype(F32)) + (q_z[2].astype(F32) + q_z[3].astype(F32))).astype(BF16)
    ret[zh, 0, x, y] = piece[:, 0:256]
    ret[zh, 1, x, y] = piece[:, 256:512]

    start(S_GZ, zh, at_z, lambda j: ret.at[zh, :, x, y], ret.at[zh, :, x, y])
    finish(S_GZ, zh, at_z, lambda j: ret.at[j, :, x, y])
    start(S_GY0, y, at_y, lambda j: ret.at[:, 0, x, y], ret.at[:, 0, x, y])
    start(S_GX1, x, at_x, lambda j: ret.at[:, 1, x, y], ret.at[:, 1, x, y])
    finish(S_GY0, y, at_y, lambda j: ret.at[:, 0, x, j])
    start(S_GX0, x, at_x, lambda j: ret.at[:, 0, x], ret.at[:, 0, x])
    finish(S_GX1, x, at_x, lambda j: ret.at[:, 1, j, y])
    start(S_GY1, y, at_y, lambda j: ret.at[:, 1, :, y], ret.at[:, 1, :, y])
    outs = []
    for half in range(2):
        if half == 0:
            finish(S_GX0, x, at_x, lambda j: ret.at[:, 0, j])
        else:
            finish(S_GY1, y, at_y, lambda j: ret.at[:, 1, :, j])
        for z in range(4):
            rhs = ret[z, half].reshape(512, 256)
            n = half * 4 + z
            out_buf[n] = jnp.dot(h_win[...], rhs, preferred_element_type=F32).astype(BF16)
            at = 512 * z + 256 * half
            cp = pltpu.make_async_copy(out_buf.at[n], out_hbm.at[:, at:at + 256], osem.at[n])
            cp.start()
            outs.append(cp)
    for cp in sends:
        cp.wait_send()
    for cp in outs:
        cp.wait()


def per_device(cotangent, activations, shard_of_token, shard_weight, hidden_basis, input_basis, eigenvalues, panel_order):
    vmem = pl.BlockSpec(memory_space=pltpu.VMEM)
    hbm = pl.BlockSpec(memory_space=pltpu.HBM)

    def buf(*shape):
        return pltpu.VMEM(shape, BF16)

    h_src, e_src = pl.pallas_call(
        pick,
        out_shape=[jax.ShapeDtypeStruct((448, 512), BF16), jax.ShapeDtypeStruct((512, 128), BF16)],
        in_specs=[hbm, hbm, hbm],
        out_specs=[vmem, vmem],
        scratch_shapes=[pltpu.SMEM((2,), jnp.int32), pltpu.SemaphoreType.DMA((5,))],
        name="pick",
    )(panel_order, hidden_basis, eigenvalues)

    return pl.pallas_call(
        kernel,
        out_shape=jax.ShapeDtypeStruct((448, 2048), BF16),
        in_specs=[hbm, hbm, hbm, hbm, hbm, vmem, vmem],
        out_specs=hbm,
        scratch_shapes=[
            buf(448, 256), buf(256, 448), pltpu.VMEM((1, 256), jnp.int32), pltpu.VMEM((16, 128), F32),
            buf(4, 256, 128), buf(4, 2048, 128),
            buf(4, 128, 128), buf(4, 128, 128),
            buf(224, 512), buf(224, 512), buf(448, 512),
            buf(4, 256, 128), buf(4, 256, 128), buf(4, 64, 128), buf(4, 64, 128), buf(64, 128), buf(4, 64, 128), buf(4, 64, 128),
            buf(128, 512), buf(4, 128, 512), buf(4, 128, 512),
            buf(4, 128, 128), buf(4, 128, 128), buf(4, 128, 128),
            buf(4, 4, 32, 512), buf(4, 4, 32, 512), buf(4, 32, 512), buf(4, 32, 512), buf(4, 2, 4, 4, 32, 256),
            buf(8, 448, 256),
            pltpu.SemaphoreType.DMA((N_STAGES, 4)),
            pltpu.SemaphoreType.DMA((N_STAGES, 4)),
            pltpu.SemaphoreType.DMA((5,)),
            pltpu.SemaphoreType.DMA((8,)),
        ],
        compiler_params=pltpu.CompilerParams(
            collective_id=0, has_side_effects=True, vmem_limit_bytes=48 * 1024 * 1024),
        cost_estimate=pl.CostEstimate(flops=3_000_000_000, bytes_accessed=12_000_000, transcendentals=0),
        name="influence",
    )(
        cotangent.T, activations, shard_of_token.reshape(1, 256), shard_weight.reshape(16, 128),
        input_basis, h_src, e_src,
    )


def solution(mesh):
    placed = (
        P("col", "row"),
        P("col", "row"),
        P("col"),
        P(),
        P("row", "col"),
        P("col", "row"),
        P("col", "row"),
        P(),
    )
    return jax.shard_map(
        per_device, mesh=mesh, in_specs=placed, out_specs=P("row", "col"), check_vma=False
    )
```

```python
import jax
import jax.numpy as jnp
from jax import lax
from jax.experimental import pallas as pl
from jax.experimental.pallas import tpu as pltpu
from jax.sharding import PartitionSpec as P

PANEL = 256
LAST = 111
PER_COL = 28
DAMPING = 0.01
MESH = pl.DeviceIdType.MESH
F32 = jnp.float32
BF16 = jnp.bfloat16

(R_TURN, R_ACT, R_ASIB, R_BAS, R_SIB, R_EIX, R_EIC, R_H, R_HL, R_PY, R_PX, R_PZ, R_PG, R_RY, R_RZ, R_RG, R_TC, R_QY, R_QZ,
 R_GZ, R_GX, R_GY, R_FX, R_FY) = (
    0, 1, 5, 9, 13, 17, 21, 25, 28, 30, 38, 42, 46, 50, 54, 58, 74, 75, 91, 95, 103, 107, 111, 127)
N_RECV = 143
N_SEND = 144


def pick(order_hbm, hid_hbm, eig_hbm, h_src, e_src, order, sems):
    col = lax.axis_index("col")
    cp = pltpu.make_async_copy(order_hbm, order, sems.at[0])
    cp.start()
    cp.wait()
    other = order[0] + order[1] - LAST
    place = pl.multiple_of((other - col * PER_COL) * PANEL, PANEL)
    mine = (other >= col * PER_COL) & (other < (col + 1) * PER_COL)
    end = (PER_COL - 1) * PANEL

    def fetch(have, at, k):
        h_part = h_src.at[k]
        e_part = e_src.at[PANEL * k:PANEL * (k + 1)]

        def copies():
            return (pltpu.make_async_copy(hid_hbm.at[:, pl.ds(at, PANEL)], h_part, sems.at[1 + 2 * k]),
                    pltpu.make_async_copy(eig_hbm.at[pl.ds(at, PANEL)], e_part, sems.at[2 + 2 * k]))

        @pl.when(have)
        def _():
            for cp in copies():
                cp.start()

        @pl.when(jnp.logical_not(have))
        def _():
            h_part[...] = jnp.zeros(h_part.shape, BF16)
            e_part[...] = jnp.zeros(e_part.shape, BF16)

        def settle():
            @pl.when(have)
            def _():
                for cp in copies():
                    cp.wait()
        return settle

    settle = [fetch(mine, place, 0), fetch(col == 3, end, 1)]
    for wait in settle:
        wait()


def add4(a, b, c, d):
    return (a.astype(F32) + b.astype(F32)) + (c.astype(F32) + d.astype(F32))


def kernel(
    cot_hbm, act_hbm, shard_hbm, weight_hbm, bas_hbm, h_src, e_src, out_ref,
    cot_t, cot, shard_ref, weight_ref, act_g, bas_g,
    e_x, e_c,
    h_a, h_b, h_win,
    p_src, p_y, p_x0, p_x, p_z0, p_z, p_s, p_g,
    pk, r_src, r_y, r_full,
    t_src, t_in, c_all,
    q_src, q_y, q_z0, q_z, g_src, ret,
    ssem, rsem, lsem,
):
    row = lax.axis_index("row")
    col = lax.axis_index("col")
    x = row % 4
    zh = (row // 4) % 4
    y = row // 16
    core = col % 2
    zlo = col // 2

    def at_x(j):
        return (y * 16 + zh * 4 + j, col)

    def at_y(j):
        return (j * 16 + zh * 4 + x, col)

    def at_z(j):
        return (y * 16 + j * 4 + x, col)

    def at_c(j):
        return (row, j)

    def at_yc(j, k):
        return (j * 16 + zh * 4 + x, k)

    sibling = at_c(zlo * 2 + 1 - core)
    partner = at_c((col + 2) % 4)

    sends = []
    used = [0]

    def copy(src, dst, recv, device):
        cp = pltpu.make_async_remote_copy(
            src_ref=src, dst_ref=dst, send_sem=ssem.at[used[0]], recv_sem=rsem.at[recv],
            device_id=device, device_id_type=MESH)
        used[0] += 1
        cp.start()
        return cp

    def send(src, dst, recv, device):
        sends.append(copy(src, dst, recv, device))

    def arrived(recv, dst):
        pltpu.make_async_remote_copy(
            src_ref=dst, dst_ref=dst, send_sem=ssem.at[0], recv_sem=rsem.at[recv],
            device_id=sibling, device_id_type=MESH).wait_recv()

    def start(base, me, place, src_of, dst):
        for d in (2, 1, 3):
            j = (me + d) % 4
            send(src_of(j), dst, base + me, place(j))

    def finish(base, me, dst_of):
        for d in (1, 3, 2):
            j = (me + d) % 4
            arrived(base + j, dst_of(j))

    barrier = pltpu.get_barrier_semaphore()
    for d in (1, 2, 3):
        pl.semaphore_signal(barrier, inc=1, device_id=at_c((col + d) % 4), device_id_type=MESH)
    for me, place in ((x, at_x), (y, at_y), (zh, at_z)):
        for d in (2, 1, 3):
            pl.semaphore_signal(barrier, inc=1, device_id=place((me + d) % 4), device_id_type=MESH)
    for d in (2, 1, 3):
        pl.semaphore_signal(
            barrier, inc=1, device_id=(at_z((zh + d) % 4)[0], zlo * 2 + 1 - core), device_id_type=MESH)


    @pl.when(col != y)
    def _():
        for d in (2, 1, 3):
            pl.semaphore_signal(barrier, inc=1, device_id=at_yc((y + d) % 4, y), device_id_type=MESH)

    loads = [
        pltpu.make_async_copy(shard_hbm, shard_ref, lsem.at[0]),
        pltpu.make_async_copy(weight_hbm, weight_ref, lsem.at[1]),
        pltpu.make_async_copy(cot_hbm, cot_t, lsem.at[2]),
        pltpu.make_async_copy(bas_hbm, bas_g.at[core, x], lsem.at[3]),
    ]
    for cp in loads:
        cp.start()

    pl.semaphore_wait(barrier, jnp.where(col == y, 15, 18))

    keep = pl.multiple_of(core * 224, 224)
    give = pl.multiple_of((1 - core) * 224, 224)
    holder = col == 3

    def last_copies(n):
        return [pltpu.make_async_remote_copy(
            src_ref=src, dst_ref=src_to, send_sem=ssem.at[n + i], recv_sem=rsem.at[R_HL],
            device_id=at_c(k), device_id_type=MESH)
            for i, (src, src_to, k) in enumerate((
                (h_src.at[1, 0:224], h_win.at[1, 0:224], 0),
                (h_src.at[1, 224:448], h_win.at[1, 224:448], 1),
                (h_src.at[1], h_win.at[1], 2)))]

    first_last = used[0]
    used[0] += 3

    @pl.when(holder)
    def _():
        for cp in last_copies(first_last):
            cp.start()
        cp = pltpu.make_async_copy(h_src.at[1], h_win.at[1], lsem.at[5])
        cp.start()
        cp.wait()

    send(h_src.at[0, pl.ds(give, 224)], h_a, R_H, sibling)

    swap = used[0]

    @pl.when(col != y)
    def _():
        copy(act_hbm, act_g.at[y % 2, x], R_TURN, at_yc(col, y))

    @pl.when(col == y)
    def _():
        cp = pltpu.make_async_copy(act_hbm, act_g.at[core, x], lsem.at[4])
        cp.start()
        cp.wait()

    loads[0].wait()
    loads[1].wait()
    ids = jnp.transpose(jnp.broadcast_to(shard_ref[...].astype(F32), (128, 256)))
    lane = lax.broadcasted_iota(jnp.int32, (256, 128), 1).astype(F32)
    weight = jnp.zeros((256, 128), F32)
    for j in range(16):
        weight = weight + jnp.where(ids == lane + float(128 * j), weight_ref[j:j + 1, :], 0.0)
    weight = jnp.sum(weight, axis=1, keepdims=True)

    arrived(R_H, h_a)
    h_a[...] = h_a[...] + h_src[0, pl.ds(keep, 224)]
    send(h_a, h_b, R_H + 1, partner)
    x_up, x_down, x_far = (x + 1) % 4, (x + 3) % 4, (x + 2) % 4
    send(bas_hbm, bas_g.at[core, x], R_BAS + 0, at_x(x_up))
    send(bas_hbm, bas_g.at[core, x], R_BAS + 1, at_x(x_down))
    loads[2].wait()
    cot[...] = (jnp.transpose(cot_t[...].astype(F32)) * weight).astype(BF16)

    def project(p):
        part = jnp.dot(cot[...], h_win[p], preferred_element_type=F32).astype(BF16)
        for j in range(4):
            p_src[p, j] = part[64 * j:64 * (j + 1)]
        start(R_PY + 4 * p, y, at_y, lambda j: p_src.at[p, j], p_y.at[p, y])
        p_y[p, y] = p_src[p, y]

    @pl.when(zlo == 0)
    def _():
        arrived(R_HL, h_win.at[1, pl.ds(keep, 224)])
        cp = copy(h_win.at[1, pl.ds(keep, 224)], h_win.at[1, pl.ds(keep, 224)], R_HL + 1, sibling)
        arrived(R_HL + 1, h_win.at[1, pl.ds(give, 224)])
        cp.wait_send()

    @pl.when(col == 2)
    def _():
        arrived(R_HL, h_win.at[1])

    project(1)
    arrived(R_H + 1, h_b)
    h_win[0, pl.ds(keep, 224)] = h_a[...] + h_b[...]
    send(h_win.at[0, pl.ds(keep, 224)], h_win.at[0, pl.ds(keep, 224)], R_H + 2, sibling)

    @pl.when(col != y)
    def _():
        arrived(R_TURN, act_g.at[core, x])
    start(R_ACT, x, at_x, lambda j: act_g.at[core, x], act_g.at[core, x])
    send(act_g.at[core, x], act_g.at[core, x], R_ASIB + x, sibling)

    arrived(R_H + 2, h_win.at[0, pl.ds(give, 224)])
    project(0)

    @pl.when(holder)
    def _():
        for cp in last_copies(first_last):
            cp.wait_send()

    for p in (1, 0):
        finish(R_PY + 4 * p, y, lambda j: p_y.at[p, j])
        total = add4(p_y[p, 0], p_y[p, 1], p_y[p, 2], p_y[p, 3]).astype(BF16)
        for j in range(2):
            p_x0[2 * p + j] = total[:, 128 * j:128 * (j + 1)]
    start(R_PX, x, at_x, lambda j: p_x0.at[j], p_x.at[x])
    p_x[x] = p_x0[x]
    e_x[x] = e_src[pl.ds(pl.multiple_of(128 * x, 128), 128)]
    start(R_EIX, x, at_x, lambda j: e_src.at[pl.ds(pl.multiple_of(128 * j, 128), 128)], e_x.at[x])
    finish(R_PX, x, lambda j: p_x.at[j])
    p_z0[...] = add4(p_x[0], p_x[1], p_x[2], p_x[3]).astype(BF16)
    start(R_PZ, zh, at_z, lambda j: p_z0, p_z.at[zh])
    p_z[zh] = p_z0[...]
    for d in (1, 3, 2):
        j = (x + d) % 4
        arrived(R_ACT + j, act_g.at[core, j])
        send(act_g.at[core, j], act_g.at[core, j], R_ASIB + j, sibling)

    arrived(R_BAS + 0, bas_g.at[core, x_down])
    send(bas_g.at[core, x_down, 0:1024], bas_g.at[core, x_down, 0:1024], R_BAS + 2, at_x(x_up))
    arrived(R_BAS + 1, bas_g.at[core, x_up])
    send(bas_g.at[core, x_up, 1024:2048], bas_g.at[core, x_up, 1024:2048], R_BAS + 3, at_x(x_down))

    finish(R_PZ, zh, lambda j: p_z.at[j])
    p_s[...] = add4(p_z[0], p_z[1], p_z[2], p_z[3]).astype(BF16)
    first_turn = used[0]
    used[0] += 4

    def turn(k):
        return pltpu.make_async_remote_copy(
            src_ref=p_s, dst_ref=p_g.at[y], send_sem=ssem.at[first_turn + k], recv_sem=rsem.at[R_PG + y],
            device_id=at_yc(col, k), device_id_type=MESH)

    for k in range(4):
        away = (col != y) | (col != k)

        @pl.when(away)
        def _():
            turn(k).start()

        @pl.when(jnp.logical_not(away))
        def _():
            p_g[y] = p_s[...]

    finish(R_EIX, x, lambda j: e_x.at[j])
    for d in (2, 1, 3):
        j = (col + d) % 4
        half = pl.ds(pl.multiple_of(64 * (j % 2), 64), 64)
        send(e_x.at[:, half], e_c.at[col], R_EIC + col, at_c(j))
    e_c[col] = e_x[:, pl.ds(pl.multiple_of(64 * core, 64), 64)]
    for j in range(4):
        arrived(R_ASIB + j, act_g.at[1 - core, j])
    for j in range(4):
        @pl.when((col != y) | (j != y))
        def _():
            arrived(R_PG + j, p_g.at[j])

    turned_p = jnp.transpose(p_g[...].reshape(256, 128).astype(F32)).astype(BF16)
    pk[0] = turned_p[0:64]
    pk[1] = turned_p[64:128]
    mine = pk[core]
    for q in range(2):
        for j in range(4):
            part = jnp.dot(mine, act_g[q, j], preferred_element_type=F32).astype(BF16)
            for k in range(4):
                r_src[k, q, :, 128 * j:128 * (j + 1)] = part[16 * k:16 * (k + 1)]
    start(R_RY, y, at_y, lambda j: r_src.at[j], r_y.at[y])
    r_y[y] = r_src[y]
    send(bas_hbm, bas_g.at[core, x], R_SIB + 0, sibling)
    send(bas_g.at[core, x_down], bas_g.at[core, x_down], R_SIB + 1, sibling)
    send(bas_g.at[core, x_up], bas_g.at[core, x_up], R_SIB + 2, sibling)
    finish(R_RY, y, lambda j: r_y.at[j])
    here = pl.ds(pl.multiple_of(16 * y, 16), 16)
    r_full[zh, :, here] = add4(r_y[0], r_y[1], r_y[2], r_y[3]).astype(BF16)
    start(R_RZ, zh, at_z, lambda j: r_full.at[zh, :, here], r_full.at[zh, :, here])
    start(R_RG + 4 * zh, y, at_y, lambda j: r_full.at[zh, :, here], r_full.at[zh, :, here])
    arrived(R_BAS + 2, bas_g.at[core, x_far, 0:1024])
    arrived(R_BAS + 3, bas_g.at[core, x_far, 1024:2048])
    send(bas_g.at[core, x_far], bas_g.at[core, x_far], R_SIB + 3, sibling)
    for d in (1, 3, 2):
        z = (zh + d) % 4
        arrived(R_RZ + z, r_full.at[z, :, here])
        start(R_RG + 4 * z, y, at_y, lambda j: r_full.at[z, :, here], r_full.at[z, :, here])
    for d in (0, 1, 3, 2):
        z = (zh + d) % 4
        for e in (1, 3, 2):
            j = (y + e) % 4
            arrived(R_RG + 4 * z + j, r_full.at[z, :, pl.ds(pl.multiple_of(16 * j, 16), 16)])

    for k in range(4):
        @pl.when((col != y) | (col != k))
        def _():
            turn(k).wait_send()

    loads[3].wait()
    for j, slot in ((0, x), (1, x_down), (2, x_up), (3, x_far)):
        arrived(R_SIB + j, bas_g.at[1 - core, slot])
    own = []
    for j in range(4):
        acc = None
        for q in range(2):
            for z in range(4):
                term = jnp.dot(r_full[z, q], bas_g[q, j, 512 * z:512 * (z + 1)], preferred_element_type=F32)
                acc = term if acc is None else acc + term
        own.append(acc)
        t_src[j] = acc.astype(BF16)
    send(t_src, t_in, R_TC, partner)
    finish(R_EIC, col, lambda j: e_c.at[j])
    damped = add4(e_c[0], e_c[1], e_c[2], e_c[3]) + DAMPING
    arrived(R_TC, t_in)
    for j in range(4):
        c_all[j] = ((own[j] + t_in[j].astype(F32)) / damped[j]).astype(BF16)

    z_order = [(zh + d) % 4 for d in (2, 1, 3, 0)]
    for z in z_order:
        for q in range(2):
            acc = None
            for j in range(4):
                term = lax.dot_general(
                    c_all[j], bas_g[q, j, pl.ds(pl.multiple_of(512 * z, 512), 512)], (((1,), (1,)), ((), ())),
                    preferred_element_type=F32)
                acc = term if acc is None else acc + term
            acc = acc.astype(BF16)
            for j in range(4):
                q_src[j, z, q] = acc[16 * j:16 * (j + 1)]
        for d in (2, 1, 3):
            j = (y + d) % 4
            send(q_src.at[j, z], q_y.at[y, z], R_QY + 4 * y + z, at_y(j))
        q_y[y, z] = q_src[y, z]
    for n, z in enumerate(z_order):
        for d in (1, 3, 2):
            j = (y + d) % 4
            arrived(R_QY + 4 * j + z, q_y.at[j, z])
        total = add4(q_y[0, z], q_y[1, z], q_y[2, z], q_y[3, z]).astype(BF16)
        if n < 3:
            q_z0[z] = total
            send(q_z0.at[z], q_z.at[zh], R_QZ + zh, at_z(z))
        else:
            q_z[zh] = total
    finish(R_QZ, zh, lambda j: q_z.at[j])
    piece = add4(q_z[0], q_z[1], q_z[2], q_z[3]).astype(BF16)

    for half in range(2):
        g_src[:, half] = piece[:, :, 256 * half:256 * (half + 1)]
    ret[zh, :, x, core, y] = g_src[core]
    for d in (2, 1, 3):
        j = (zh + d) % 4
        for k in (core, 1 - core):
            send(g_src.at[k], ret.at[zh, :, x, core, y], R_GZ + 2 * zh + core, (at_z(j)[0], zlo * 2 + k))
    send(g_src.at[1 - core], ret.at[zh, :, x, core, y], R_GZ + 2 * zh + core, sibling)
    arrived(R_GZ + 2 * zh + 1 - core, ret.at[zh, :, x, 1 - core, y])
    for d in (1, 3, 2):
        j = (zh + d) % 4
        for k in range(2):
            arrived(R_GZ + 2 * j + k, ret.at[j, :, x, k, y])

    start(R_GX, x, at_x, lambda j: ret.at[:, :, x, :, y], ret.at[:, :, x, :, y])
    start(R_GY, y, at_y, lambda j: ret.at[:, :, x, :, y], ret.at[:, :, x, :, y])
    for d in (1, 3, 2):
        j = (y + d) % 4
        arrived(R_GY + j, ret.at[:, :, x, :, j])
        for e in (2, 1, 3):
            send(ret.at[:, 0, x, :, j], ret.at[:, 0, x, :, j], R_FX + 4 * x + j, at_x((x + e) % 4))
        j = (x + d) % 4
        arrived(R_GX + j, ret.at[:, :, j, :, y])
        for e in (2, 1, 3):
            send(ret.at[:, 1, j, :, y], ret.at[:, 1, j, :, y], R_FY + 4 * j + y, at_y((y + e) % 4))
    for half in range(2):
        for d in (1, 3, 2):
            for e in (1, 3, 2):
                jx, jy = (x + e) % 4, (y + d) % 4
                arrived((R_FX if half == 0 else R_FY) + 4 * jx + jy, ret.at[:, half, jx, :, jy])
        for z in range(4):
            acc = jnp.dot(h_win[0], ret[z, half, 0:2].reshape(256, 256), preferred_element_type=F32)
            acc = acc + jnp.dot(h_win[1], ret[z, half, 2:4].reshape(256, 256), preferred_element_type=F32)
            at = 512 * z + 256 * half
            out_ref[:, at:at + 256] = acc.astype(BF16)
    for cp in sends:
        cp.wait_send()

    @pl.when(col != y)
    def _():
        pltpu.make_async_remote_copy(
            src_ref=act_hbm, dst_ref=act_g.at[y % 2, x], send_sem=ssem.at[swap], recv_sem=rsem.at[R_TURN],
            device_id=at_yc(col, y), device_id_type=MESH).wait_send()


def per_device(cotangent, activations, shard_of_token, shard_weight, hidden_basis, input_basis, eigenvalues, panel_order):
    vmem = pl.BlockSpec(memory_space=pltpu.VMEM)
    hbm = pl.BlockSpec(memory_space=pltpu.HBM)

    def buf(*shape):
        return pltpu.VMEM(shape, BF16)

    h_src, e_src = pl.pallas_call(
        pick,
        out_shape=[jax.ShapeDtypeStruct((2, 448, 256), BF16), jax.ShapeDtypeStruct((512, 128), BF16)],
        in_specs=[hbm, hbm, hbm],
        out_specs=[vmem, vmem],
        scratch_shapes=[pltpu.SMEM((2,), jnp.int32), pltpu.SemaphoreType.DMA((5,))],
        compiler_params=pltpu.CompilerParams(vmem_limit_bytes=60 * 1024 * 1024),
        name="pick",
    )(panel_order, hidden_basis, eigenvalues)

    return pl.pallas_call(
        kernel,
        out_shape=jax.ShapeDtypeStruct((448, 2048), BF16),
        in_specs=[hbm, hbm, hbm, hbm, hbm, vmem, vmem],
        out_specs=vmem,
        scratch_shapes=[
            buf(448, 256), buf(256, 448), pltpu.VMEM((1, 256), jnp.int32), pltpu.VMEM((16, 128), F32),
            buf(2, 4, 256, 128), buf(2, 4, 2048, 128),
            buf(4, 128, 128), buf(4, 4, 64, 128),
            buf(224, 256), buf(224, 256), buf(2, 448, 256),
            buf(2, 4, 64, 256), buf(2, 4, 64, 256), buf(4, 64, 128), buf(4, 64, 128), buf(64, 128), buf(4, 64, 128),
            buf(64, 128), buf(4, 64, 128),
            buf(2, 64, 256), buf(4, 2, 16, 512), buf(4, 2, 16, 512), buf(4, 2, 64, 512),
            buf(4, 64, 128), buf(4, 64, 128), buf(4, 64, 128),
            buf(4, 4, 2, 16, 512), buf(4, 4, 2, 16, 512), buf(4, 2, 16, 512), buf(4, 2, 16, 512), buf(2, 2, 16, 256),
            buf(4, 2, 4, 2, 4, 16, 256),
            pltpu.SemaphoreType.DMA((N_SEND,)),
            pltpu.SemaphoreType.DMA((N_RECV,)),
            pltpu.SemaphoreType.DMA((6,)),
        ],
        compiler_params=pltpu.CompilerParams(
            collective_id=0, has_side_effects=True, vmem_limit_bytes=60 * 1024 * 1024),
        cost_estimate=pl.CostEstimate(flops=3_000_000_000, bytes_accessed=12_000_000, transcendentals=0),
        name="influence",
    )(
        cotangent.T, activations, shard_of_token.reshape(1, 256), shard_weight.reshape(16, 128),
        input_basis, h_src, e_src,
    )


def solution(mesh):
    placed = (
        P("col", "row"),
        P("col", "row"),
        P("col"),
        P(),
        P("row", "col"),
        P("col", "row"),
        P("col", "row"),
        P(),
    )
    return jax.shard_map(
        per_device, mesh=mesh, in_specs=placed, out_specs=P("row", "col"), check_vma=False
    )
```

```python
import jax
import jax.numpy as jnp
from jax import lax
from jax.experimental import pallas as pl
from jax.experimental.pallas import tpu as pltpu
from jax.sharding import PartitionSpec as P

PANEL = 256
LAST = 111
PER_COL = 28
DAMPING = 0.01
MESH = pl.DeviceIdType.MESH
F32 = jnp.float32
BF16 = jnp.bfloat16

(R_TURN, R_ACT, R_ASIB, R_BAS, R_SIB, R_EIX, R_EIC, R_H, R_HL, R_PY, R_PX, R_PZ, R_PG, R_RY, R_RZ, R_RG, R_TC, R_QY, R_QZ,
 R_GZ, R_GX, R_GY, R_FX, R_FY) = (
    0, 1, 5, 9, 15, 19, 23, 27, 30, 32, 40, 44, 48, 52, 56, 60, 76, 77, 93, 97, 105, 109, 113, 125)
N_RECV = 137
N_SEND = 160


def pick(order_hbm, hid_hbm, eig_hbm, h_src, e_src, order, sems):
    col = lax.axis_index("col")
    cp = pltpu.make_async_copy(order_hbm, order, sems.at[0])
    cp.start()
    cp.wait()
    other = order[0] + order[1] - LAST
    place = pl.multiple_of((other - col * PER_COL) * PANEL, PANEL)
    mine = (other >= col * PER_COL) & (other < (col + 1) * PER_COL)
    end = (PER_COL - 1) * PANEL

    def fetch(have, at, k):
        h_part = h_src.at[k]
        e_part = e_src.at[PANEL * k:PANEL * (k + 1)]

        def copies():
            return (pltpu.make_async_copy(hid_hbm.at[:, pl.ds(at, PANEL)], h_part, sems.at[1 + 2 * k]),
                    pltpu.make_async_copy(eig_hbm.at[pl.ds(at, PANEL)], e_part, sems.at[2 + 2 * k]))

        @pl.when(have)
        def _():
            for cp in copies():
                cp.start()

        @pl.when(jnp.logical_not(have))
        def _():
            h_part[...] = jnp.zeros(h_part.shape, BF16)
            e_part[...] = jnp.zeros(e_part.shape, BF16)

        def settle():
            @pl.when(have)
            def _():
                for cp in copies():
                    cp.wait()
        return settle

    settle = [fetch(mine, place, 0), fetch(col == 3, end, 1)]
    for wait in settle:
        wait()


def add4(a, b, c, d):
    return (a.astype(F32) + b.astype(F32)) + (c.astype(F32) + d.astype(F32))


def kernel(
    cot_hbm, act_hbm, shard_hbm, weight_hbm, bas_hbm, h_src, e_src, ret, win_out,
    cot_t, cot, shard_ref, weight_ref, act_g, bas_g,
    e_x, e_c,
    h_keep, h_a, h_b, h_win,
    p_src, p_y, p_x0, p_x, p_z0, p_z, p_s, p_g,
    pk, r_src, r_y, r_full,
    t_src, t_in, c_all,
    q_src, q_y, q_z0, q_z, g_src,
    ssem, rsem, lsem,
):
    row = lax.axis_index("row")
    col = lax.axis_index("col")
    x = row % 4
    zh = (row // 4) % 4
    y = row // 16
    core = col % 2
    zlo = col // 2

    def at_x(j):
        return (y * 16 + zh * 4 + j, col)

    def at_y(j):
        return (j * 16 + zh * 4 + x, col)

    def at_z(j):
        return (y * 16 + j * 4 + x, col)

    def at_c(j):
        return (row, j)

    def at_yc(j, k):
        return (j * 16 + zh * 4 + x, k)

    sibling = at_c(zlo * 2 + 1 - core)
    partner = at_c((col + 2) % 4)

    sends = []
    used = [0]

    def copy(src, dst, recv, device):
        cp = pltpu.make_async_remote_copy(
            src_ref=src, dst_ref=dst, send_sem=ssem.at[used[0]], recv_sem=rsem.at[recv],
            device_id=device, device_id_type=MESH)
        used[0] += 1
        cp.start()
        return cp

    def send(src, dst, recv, device):
        sends.append(copy(src, dst, recv, device))

    def arrived(recv, dst):
        pltpu.make_async_remote_copy(
            src_ref=dst, dst_ref=dst, send_sem=ssem.at[0], recv_sem=rsem.at[recv],
            device_id=sibling, device_id_type=MESH).wait_recv()

    def start(base, me, place, src_of, dst):
        for d in (2, 1, 3):
            j = (me + d) % 4
            send(src_of(j), dst, base + me, place(j))

    def finish(base, me, dst_of):
        for d in (1, 3, 2):
            j = (me + d) % 4
            arrived(base + j, dst_of(j))

    barrier = pltpu.get_barrier_semaphore()
    for d in (1, 2, 3):
        pl.semaphore_signal(barrier, inc=1, device_id=at_c((col + d) % 4), device_id_type=MESH)
    for me, place in ((x, at_x), (y, at_y), (zh, at_z)):
        for d in (2, 1, 3):
            pl.semaphore_signal(barrier, inc=1, device_id=place((me + d) % 4), device_id_type=MESH)
    for d in (2, 1, 3):
        pl.semaphore_signal(
            barrier, inc=1, device_id=(at_z((zh + d) % 4)[0], zlo * 2 + 1 - core), device_id_type=MESH)


    @pl.when(col != y)
    def _():
        for d in (2, 1, 3):
            pl.semaphore_signal(barrier, inc=1, device_id=at_yc((y + d) % 4, y), device_id_type=MESH)

    keep = pl.multiple_of(core * 224, 224)
    give = pl.multiple_of((1 - core) * 224, 224)
    loads = [
        pltpu.make_async_copy(shard_hbm, shard_ref, lsem.at[0]),
        pltpu.make_async_copy(weight_hbm, weight_ref, lsem.at[1]),
        pltpu.make_async_copy(cot_hbm, cot_t, lsem.at[2]),
        pltpu.make_async_copy(bas_hbm, bas_g.at[core, x], lsem.at[3]),
        pltpu.make_async_copy(h_src.at[0, pl.ds(keep, 224)], h_keep, lsem.at[4]),
        pltpu.make_async_copy(e_src.at[pl.ds(pl.multiple_of(128 * x, 128), 128)], e_x.at[x], lsem.at[5]),
    ]
    for cp in loads:
        cp.start()

    pl.semaphore_wait(barrier, jnp.where(col == y, 15, 18))

    holder = col == 3

    def last_copies(n):
        return [pltpu.make_async_remote_copy(
            src_ref=src, dst_ref=src_to, send_sem=ssem.at[n + i], recv_sem=rsem.at[R_HL],
            device_id=at_c(k), device_id_type=MESH)
            for i, (src, src_to, k) in enumerate((
                (h_src.at[1, 0:224], h_win.at[1, 0:224], 0),
                (h_src.at[1, 224:448], h_win.at[1, 224:448], 1),
                (h_src.at[1], h_win.at[1], 2)))]

    first_last = used[0]
    used[0] += 3

    @pl.when(holder)
    def _():
        for cp in last_copies(first_last):
            cp.start()
        cp = pltpu.make_async_copy(h_src.at[1], h_win.at[1], lsem.at[7])
        cp.start()
        cp.wait()

    send(h_src.at[0, pl.ds(give, 224)], h_a, R_H, sibling)

    swap = used[0]

    @pl.when(col != y)
    def _():
        copy(act_hbm, act_g.at[y % 2, x], R_TURN, at_yc(col, y))

    @pl.when(col == y)
    def _():
        cp = pltpu.make_async_copy(act_hbm, act_g.at[core, x], lsem.at[6])
        cp.start()
        cp.wait()

    loads[0].wait()
    loads[1].wait()
    ids = jnp.transpose(jnp.broadcast_to(shard_ref[...].astype(F32), (128, 256)))
    lane = lax.broadcasted_iota(jnp.int32, (256, 128), 1).astype(F32)
    weight = jnp.zeros((256, 128), F32)
    for j in range(16):
        weight = weight + jnp.where(ids == lane + float(128 * j), weight_ref[j:j + 1, :], 0.0)
    weight = jnp.sum(weight, axis=1, keepdims=True)

    arrived(R_H, h_a)
    loads[4].wait()
    h_a[...] = h_a[...] + h_keep[...]
    send(h_a, h_b, R_H + 1, partner)
    x_up, x_down, x_far = (x + 1) % 4, (x + 3) % 4, (x + 2) % 4
    loads[2].wait()
    cot[...] = (jnp.transpose(cot_t[...].astype(F32)) * weight).astype(BF16)

    def project(p):
        part = jnp.dot(cot[...], h_win[p], preferred_element_type=F32).astype(BF16)
        for j in range(4):
            p_src[p, j] = part[64 * j:64 * (j + 1)]
        start(R_PY + 4 * p, y, at_y, lambda j: p_src.at[p, j], p_y.at[p, y])
        p_y[p, y] = p_src[p, y]

    @pl.when(zlo == 0)
    def _():
        arrived(R_HL, h_win.at[1, pl.ds(keep, 224)])
        cp = copy(h_win.at[1, pl.ds(keep, 224)], h_win.at[1, pl.ds(keep, 224)], R_HL + 1, sibling)
        arrived(R_HL + 1, h_win.at[1, pl.ds(give, 224)])
        cp.wait_send()

    @pl.when(col == 2)
    def _():
        arrived(R_HL, h_win.at[1])

    project(1)
    arrived(R_H + 1, h_b)
    h_win[0, pl.ds(keep, 224)] = h_a[...] + h_b[...]
    send(h_win.at[0, pl.ds(keep, 224)], h_win.at[0, pl.ds(keep, 224)], R_H + 2, sibling)

    @pl.when(col != y)
    def _():
        arrived(R_TURN, act_g.at[core, x])
    start(R_ACT, x, at_x, lambda j: act_g.at[core, x], act_g.at[core, x])
    send(act_g.at[core, x], act_g.at[core, x], R_ASIB + x, sibling)

    arrived(R_H + 2, h_win.at[0, pl.ds(give, 224)])
    project(0)
    wins = [pltpu.make_async_copy(h_win.at[p], win_out.at[:, PANEL * p:PANEL * (p + 1)], lsem.at[9 + p]) for p in range(2)]
    for cp in wins:
        cp.start()

    @pl.when(holder)
    def _():
        for cp in last_copies(first_last):
            cp.wait_send()

    for p in (1, 0):
        finish(R_PY + 4 * p, y, lambda j: p_y.at[p, j])
        total = add4(p_y[p, 0], p_y[p, 1], p_y[p, 2], p_y[p, 3]).astype(BF16)
        for j in range(2):
            p_x0[2 * p + j] = total[:, 128 * j:128 * (j + 1)]
    start(R_PX, x, at_x, lambda j: p_x0.at[j], p_x.at[x])
    p_x[x] = p_x0[x]
    start(R_EIX, x, at_x, lambda j: e_src.at[pl.ds(pl.multiple_of(128 * j, 128), 128)], e_x.at[x])
    finish(R_PX, x, lambda j: p_x.at[j])

    low, high = pl.ds(0, 1024), pl.ds(1024, 1024)

    def basis(slot, part, recv, j):
        send(bas_g.at[core, slot, part], bas_g.at[core, slot, part], recv, at_x(j))

    loads[3].wait()
    basis(x, low, R_BAS + 0, x_up)
    basis(x, high, R_BAS + 1, x_down)
    p_z0[...] = add4(p_x[0], p_x[1], p_x[2], p_x[3]).astype(BF16)
    start(R_PZ, zh, at_z, lambda j: p_z0, p_z.at[zh])
    p_z[zh] = p_z0[...]
    for d in (1, 3, 2):
        j = (x + d) % 4
        arrived(R_ACT + j, act_g.at[core, j])
        send(act_g.at[core, j], act_g.at[core, j], R_ASIB + j, sibling)

    basis(x, high, R_BAS + 2, x_up)
    basis(x, low, R_BAS + 3, x_down)

    finish(R_PZ, zh, lambda j: p_z.at[j])
    p_s[...] = add4(p_z[0], p_z[1], p_z[2], p_z[3]).astype(BF16)
    first_turn = used[0]
    used[0] += 4

    def turn(k):
        return pltpu.make_async_remote_copy(
            src_ref=p_s, dst_ref=p_g.at[y], send_sem=ssem.at[first_turn + k], recv_sem=rsem.at[R_PG + y],
            device_id=at_yc(col, k), device_id_type=MESH)

    for k in range(4):
        away = (col != y) | (col != k)

        @pl.when(away)
        def _():
            turn(k).start()

        @pl.when(jnp.logical_not(away))
        def _():
            p_g[y] = p_s[...]

    loads[5].wait()
    finish(R_EIX, x, lambda j: e_x.at[j])
    for d in (2, 1, 3):
        j = (col + d) % 4
        half = pl.ds(pl.multiple_of(64 * (j % 2), 64), 64)
        send(e_x.at[:, half], e_c.at[col], R_EIC + col, at_c(j))
    e_c[col] = e_x[:, pl.ds(pl.multiple_of(64 * core, 64), 64)]
    for j in range(4):
        arrived(R_ASIB + j, act_g.at[1 - core, j])
    for j in range(4):
        @pl.when((col != y) | (j != y))
        def _():
            arrived(R_PG + j, p_g.at[j])

    turned_p = jnp.transpose(p_g[...].reshape(256, 128).astype(F32)).astype(BF16)
    pk[0] = turned_p[0:64]
    pk[1] = turned_p[64:128]
    mine = pk[core]
    for q in range(2):
        for j in range(4):
            part = jnp.dot(mine, act_g[q, j], preferred_element_type=F32).astype(BF16)
            for k in range(4):
                r_src[k, q, :, 128 * j:128 * (j + 1)] = part[16 * k:16 * (k + 1)]
    start(R_RY, y, at_y, lambda j: r_src.at[j], r_y.at[y])
    r_y[y] = r_src[y]
    arrived(R_BAS + 0, bas_g.at[core, x_down, low])
    basis(x_down, low, R_BAS + 4, x_up)
    arrived(R_BAS + 1, bas_g.at[core, x_up, high])
    basis(x_up, high, R_BAS + 5, x_down)
    send(bas_g.at[core, x], bas_g.at[core, x], R_SIB + 0, sibling)
    finish(R_RY, y, lambda j: r_y.at[j])
    here = pl.ds(pl.multiple_of(16 * y, 16), 16)
    r_full[zh, :, here] = add4(r_y[0], r_y[1], r_y[2], r_y[3]).astype(BF16)
    start(R_RZ, zh, at_z, lambda j: r_full.at[zh, :, here], r_full.at[zh, :, here])
    start(R_RG + 4 * zh, y, at_y, lambda j: r_full.at[zh, :, here], r_full.at[zh, :, here])
    arrived(R_BAS + 2, bas_g.at[core, x_down, high])
    send(bas_g.at[core, x_down], bas_g.at[core, x_down], R_SIB + 1, sibling)
    arrived(R_BAS + 3, bas_g.at[core, x_up, low])
    send(bas_g.at[core, x_up], bas_g.at[core, x_up], R_SIB + 2, sibling)
    for d in (1, 3, 2):
        z = (zh + d) % 4
        arrived(R_RZ + z, r_full.at[z, :, here])
        start(R_RG + 4 * z, y, at_y, lambda j: r_full.at[z, :, here], r_full.at[z, :, here])
    arrived(R_BAS + 4, bas_g.at[core, x_far, low])
    arrived(R_BAS + 5, bas_g.at[core, x_far, high])
    send(bas_g.at[core, x_far], bas_g.at[core, x_far], R_SIB + 3, sibling)
    for d in (0, 1, 3, 2):
        z = (zh + d) % 4
        for e in (1, 3, 2):
            j = (y + e) % 4
            arrived(R_RG + 4 * z + j, r_full.at[z, :, pl.ds(pl.multiple_of(16 * j, 16), 16)])

    for k in range(4):
        @pl.when((col != y) | (col != k))
        def _():
            turn(k).wait_send()

    for j, slot in ((0, x), (1, x_down), (2, x_up), (3, x_far)):
        arrived(R_SIB + j, bas_g.at[1 - core, slot])
    own = []
    for j in range(4):
        acc = None
        for q in range(2):
            for z in range(4):
                term = jnp.dot(r_full[z, q], bas_g[q, j, 512 * z:512 * (z + 1)], preferred_element_type=F32)
                acc = term if acc is None else acc + term
        own.append(acc)
        t_src[j] = acc.astype(BF16)
    send(t_src, t_in, R_TC, partner)
    finish(R_EIC, col, lambda j: e_c.at[j])
    damped = add4(e_c[0], e_c[1], e_c[2], e_c[3]) + DAMPING
    arrived(R_TC, t_in)
    for j in range(4):
        c_all[j] = ((own[j] + t_in[j].astype(F32)) / damped[j]).astype(BF16)

    z_order = [(zh + d) % 4 for d in (2, 1, 3, 0)]
    for z in z_order:
        for q in range(2):
            acc = None
            for j in range(4):
                term = lax.dot_general(
                    c_all[j], bas_g[q, j, pl.ds(pl.multiple_of(512 * z, 512), 512)], (((1,), (1,)), ((), ())),
                    preferred_element_type=F32)
                acc = term if acc is None else acc + term
            acc = acc.astype(BF16)
            for j in range(4):
                q_src[j, z, q] = acc[16 * j:16 * (j + 1)]
        for d in (2, 1, 3):
            j = (y + d) % 4
            send(q_src.at[j, z], q_y.at[y, z], R_QY + 4 * y + z, at_y(j))
        q_y[y, z] = q_src[y, z]
    for n, z in enumerate(z_order):
        for d in (1, 3, 2):
            j = (y + d) % 4
            arrived(R_QY + 4 * j + z, q_y.at[j, z])
        total = add4(q_y[0, z], q_y[1, z], q_y[2, z], q_y[3, z]).astype(BF16)
        if n < 3:
            q_z0[z] = total
            send(q_z0.at[z], q_z.at[zh], R_QZ + zh, at_z(z))
        else:
            q_z[zh] = total
    finish(R_QZ, zh, lambda j: q_z.at[j])
    piece = add4(q_z[0], q_z[1], q_z[2], q_z[3]).astype(BF16)

    def spot(z):
        return pl.ds(pl.multiple_of(512 * z, 512), 512)

    g_src[...] = piece
    own_ret = pltpu.make_async_copy(g_src.at[core], ret.at[x, core, y, :, spot(zh)], lsem.at[8])
    own_ret.start()
    for d in (2, 1, 3):
        j = (zh + d) % 4
        for k in (core, 1 - core):
            send(g_src.at[k], ret.at[x, core, y, :, spot(zh)], R_GZ + 2 * zh + core, (at_z(j)[0], zlo * 2 + k))
    send(g_src.at[1 - core], ret.at[x, core, y, :, spot(zh)], R_GZ + 2 * zh + core, sibling)
    arrived(R_GZ + 2 * zh + 1 - core, ret.at[x, 1 - core, y, :, spot(zh)])
    for d in (1, 3, 2):
        j = (zh + d) % 4
        for k in range(2):
            arrived(R_GZ + 2 * j + k, ret.at[x, k, y, :, spot(j)])
    own_ret.wait()

    whole, part_a, part_b = 0, 1, 2
    y_up, y_down, y_far = (y + 1) % 4, (y + 3) % 4, (y + 2) % 4
    x_ring = (x, x_up, x_down, x_far, at_x)
    y_ring = (y, y_up, y_down, y_far, at_y)

    def give_both(ring, base, block):
        me, up, down, far, place = ring
        send(block(me, whole), block(me, whole), base, place(up))
        send(block(me, whole), block(me, whole), base + 1, place(down))

    def pass_on(ring, base, block, side):
        me, up, down, far, place = ring
        if side == 0:
            arrived(base, block(down, whole))
            send(block(down, part_a), block(down, part_a), base + 2, place(up))
        else:
            arrived(base + 1, block(up, whole))
            send(block(up, part_b), block(up, part_b), base + 3, place(down))

    def take_far(ring, base, block):
        me, up, down, far, place = ring
        arrived(base + 2, block(far, part_a))
        arrived(base + 3, block(far, part_b))

    def gx(j, part):
        return ret.at[j, :, y, :, (slice(0, 2048), slice(0, 1024), slice(1024, 2048))[part]]

    def gy(j, part):
        return ret.at[x, :, j, :, (slice(0, 2048), slice(0, 1024), slice(1024, 2048))[part]]

    def fx(k):
        return lambda j, part: ret.at[j, :, k, :, (slice(0, 1024), slice(0, 512), slice(512, 1024))[part]]

    def fy(k):
        return lambda j, part: ret.at[k, :, j, :, (slice(1024, 2048), slice(1024, 1536), slice(1536, 2048))[part]]

    give_both(x_ring, R_GX, gx)
    give_both(y_ring, R_GY, gy)
    near = ((0, y_down, x_down), (1, y_up, x_up))
    for side, ky, kx in near:
        pass_on(y_ring, R_GY, gy, side)
        give_both(x_ring, R_FX + 4 * side, fx(ky))
        pass_on(x_ring, R_GX, gx, side)
        give_both(y_ring, R_FY + 4 * side, fy(kx))
    take_far(y_ring, R_GY, gy)
    give_both(x_ring, R_FX + 8, fx(y_far))
    take_far(x_ring, R_GX, gx)
    give_both(y_ring, R_FY + 8, fy(x_far))
    cols = ((0, y_down, x_down), (1, y_up, x_up), (2, y_far, x_far))
    for n, ky, kx in cols:
        for side in range(2):
            pass_on(x_ring, R_FX + 4 * n, fx(ky), side)
            pass_on(y_ring, R_FY + 4 * n, fy(kx), side)
    for n, ky, kx in cols:
        take_far(x_ring, R_FX + 4 * n, fx(ky))
        take_far(y_ring, R_FY + 4 * n, fy(kx))
    for cp in wins:
        cp.wait()
    assert used[0] <= N_SEND
    for cp in sends:
        cp.wait_send()

    @pl.when(col != y)
    def _():
        pltpu.make_async_remote_copy(
            src_ref=act_hbm, dst_ref=act_g.at[y % 2, x], send_sem=ssem.at[swap], recv_sem=rsem.at[R_TURN],
            device_id=at_yc(col, y), device_id_type=MESH).wait_send()


def per_device(cotangent, activations, shard_of_token, shard_weight, hidden_basis, input_basis, eigenvalues, panel_order):
    vmem = pl.BlockSpec(memory_space=pltpu.VMEM)
    hbm = pl.BlockSpec(memory_space=pltpu.HBM)

    def buf(*shape):
        return pltpu.VMEM(shape, BF16)

    h_src, e_src = pl.pallas_call(
        pick,
        out_shape=[jax.ShapeDtypeStruct((2, 448, 256), BF16), jax.ShapeDtypeStruct((512, 128), BF16)],
        in_specs=[hbm, hbm, hbm],
        out_specs=[vmem, vmem],
        scratch_shapes=[pltpu.SMEM((2,), jnp.int32), pltpu.SemaphoreType.DMA((5,))],
        compiler_params=pltpu.CompilerParams(vmem_limit_bytes=60 * 1024 * 1024),
        name="pick",
    )(panel_order, hidden_basis, eigenvalues)

    ret, win = pl.pallas_call(
        kernel,
        out_shape=[jax.ShapeDtypeStruct((4, 2, 4, 16, 2048), BF16), jax.ShapeDtypeStruct((448, 512), BF16)],
        in_specs=[hbm] * 7,
        out_specs=[hbm, hbm],
        scratch_shapes=[
            buf(448, 256), buf(256, 448), pltpu.VMEM((1, 256), jnp.int32), pltpu.VMEM((16, 128), F32),
            buf(2, 4, 256, 128), buf(2, 4, 2048, 128),
            buf(4, 128, 128), buf(4, 4, 64, 128),
            buf(224, 256), buf(224, 256), buf(224, 256), buf(2, 448, 256),
            buf(2, 4, 64, 256), buf(2, 4, 64, 256), buf(4, 64, 128), buf(4, 64, 128), buf(64, 128), buf(4, 64, 128),
            buf(64, 128), buf(4, 64, 128),
            buf(2, 64, 256), buf(4, 2, 16, 512), buf(4, 2, 16, 512), buf(4, 2, 64, 512),
            buf(4, 64, 128), buf(4, 64, 128), buf(4, 64, 128),
            buf(4, 4, 2, 16, 512), buf(4, 4, 2, 16, 512), buf(4, 2, 16, 512), buf(4, 2, 16, 512), buf(2, 16, 512),
            pltpu.SemaphoreType.DMA((N_SEND,)),
            pltpu.SemaphoreType.DMA((N_RECV,)),
            pltpu.SemaphoreType.DMA((11,)),
        ],
        compiler_params=pltpu.CompilerParams(
            collective_id=0, has_side_effects=True, vmem_limit_bytes=50 * 1024 * 1024),
        cost_estimate=pl.CostEstimate(flops=3_000_000_000, bytes_accessed=12_000_000, transcendentals=0),
        name="influence",
    )(
        cotangent.T, activations, shard_of_token.reshape(1, 256), shard_weight.reshape(16, 128),
        input_basis, h_src, e_src,
    )

    return jnp.dot(win, ret.reshape(512, 2048), preferred_element_type=F32).astype(BF16)


def solution(mesh):
    placed = (
        P("col", "row"),
        P("col", "row"),
        P("col"),
        P(),
        P("row", "col"),
        P("col", "row"),
        P("col", "row"),
        P(),
    )
    return jax.shard_map(
        per_device, mesh=mesh, in_specs=placed, out_specs=P("row", "col"), check_vma=False
    )
```

```python
import jax
import jax.numpy as jnp
from jax import lax
from jax.experimental import pallas as pl
from jax.experimental.pallas import tpu as pltpu
from jax.sharding import PartitionSpec as P

PANEL = 256
LAST = 111
PER_COL = 28
DAMPING = 0.01
MESH = pl.DeviceIdType.MESH
F32 = jnp.float32
BF16 = jnp.bfloat16

(R_TURN, R_ACT, R_ASIB, R_BAS, R_SIB, R_EIX, R_EIC, R_H, R_HL, R_PY, R_PX, R_PZ, R_PG, R_RY, R_RZ, R_RG, R_TC, R_QY, R_QZ,
 R_GZ, R_GX, R_GY, R_FX, R_FY) = (
    0, 1, 5, 9, 15, 19, 23, 27, 30, 32, 40, 44, 48, 52, 56, 60, 76, 77, 93, 97, 105, 109, 113, 125)
N_RECV = 137
N_SEND = 160


def pick(order_hbm, hid_hbm, eig_hbm, h_src, e_src, order, sems):
    col = lax.axis_index("col")
    cp = pltpu.make_async_copy(order_hbm, order, sems.at[0])
    cp.start()
    cp.wait()
    other = order[0] + order[1] - LAST
    place = pl.multiple_of((other - col * PER_COL) * PANEL, PANEL)
    mine = (other >= col * PER_COL) & (other < (col + 1) * PER_COL)
    end = (PER_COL - 1) * PANEL

    def fetch(have, at, k):
        h_part = h_src.at[k]
        e_part = e_src.at[PANEL * k:PANEL * (k + 1)]

        def copies():
            return (pltpu.make_async_copy(hid_hbm.at[:, pl.ds(at, PANEL)], h_part, sems.at[1 + 2 * k]),
                    pltpu.make_async_copy(eig_hbm.at[pl.ds(at, PANEL)], e_part, sems.at[2 + 2 * k]))

        @pl.when(have)
        def _():
            for cp in copies():
                cp.start()

        @pl.when(jnp.logical_not(have))
        def _():
            h_part[...] = jnp.zeros(h_part.shape, BF16)
            e_part[...] = jnp.zeros(e_part.shape, BF16)

        def settle():
            @pl.when(have)
            def _():
                for cp in copies():
                    cp.wait()
        return settle

    settle = [fetch(mine, place, 0), fetch(col == 3, end, 1)]
    for wait in settle:
        wait()


def add4(a, b, c, d):
    return (a.astype(F32) + b.astype(F32)) + (c.astype(F32) + d.astype(F32))


def kernel(
    cot_hbm, act_hbm, shard_hbm, weight_hbm, bas_hbm, h_src, e_src, ret, win_out,
    cot_t, cot, shard_ref, weight_ref, act_g, bas_g,
    e_x, e_c,
    h_keep, h_a, h_b, h_win,
    p_src, p_y, p_x0, p_x, p_z0, p_z, p_s, p_g,
    pk, r_src, r_y, r_full,
    t_src, t_in, c_all,
    q_src, q_y, q_z0, q_z, g_src,
    ssem, rsem, lsem,
):
    row = lax.axis_index("row")
    col = lax.axis_index("col")
    x = row % 4
    zh = (row // 4) % 4
    y = row // 16
    core = col % 2
    zlo = col // 2

    def at_x(j):
        return (y * 16 + zh * 4 + j, col)

    def at_y(j):
        return (j * 16 + zh * 4 + x, col)

    def at_z(j):
        return (y * 16 + j * 4 + x, col)

    def at_c(j):
        return (row, j)

    def at_yc(j, k):
        return (j * 16 + zh * 4 + x, k)

    sibling = at_c(zlo * 2 + 1 - core)
    partner = at_c((col + 2) % 4)

    sends = []
    used = [0]

    def copy(src, dst, recv, device):
        cp = pltpu.make_async_remote_copy(
            src_ref=src, dst_ref=dst, send_sem=ssem.at[used[0]], recv_sem=rsem.at[recv],
            device_id=device, device_id_type=MESH)
        used[0] += 1
        cp.start()
        return cp

    def send(src, dst, recv, device):
        sends.append(copy(src, dst, recv, device))

    def arrived(recv, dst):
        pltpu.make_async_remote_copy(
            src_ref=dst, dst_ref=dst, send_sem=ssem.at[0], recv_sem=rsem.at[recv],
            device_id=sibling, device_id_type=MESH).wait_recv()

    def start(base, me, place, src_of, dst):
        for d in (2, 1, 3):
            j = (me + d) % 4
            send(src_of(j), dst, base + me, place(j))

    def finish(base, me, dst_of):
        for d in (1, 3, 2):
            j = (me + d) % 4
            arrived(base + j, dst_of(j))

    barrier = pltpu.get_barrier_semaphore()
    for d in (1, 2, 3):
        pl.semaphore_signal(barrier, inc=1, device_id=at_c((col + d) % 4), device_id_type=MESH)
    for me, place in ((x, at_x), (y, at_y), (zh, at_z)):
        for d in (2, 1, 3):
            pl.semaphore_signal(barrier, inc=1, device_id=place((me + d) % 4), device_id_type=MESH)
    for d in (2, 1, 3):
        pl.semaphore_signal(
            barrier, inc=1, device_id=(at_z((zh + d) % 4)[0], zlo * 2 + 1 - core), device_id_type=MESH)


    @pl.when(col != y)
    def _():
        for d in (2, 1, 3):
            pl.semaphore_signal(barrier, inc=1, device_id=at_yc((y + d) % 4, y), device_id_type=MESH)

    keep = pl.multiple_of(core * 224, 224)
    give = pl.multiple_of((1 - core) * 224, 224)
    loads = [
        pltpu.make_async_copy(shard_hbm, shard_ref, lsem.at[0]),
        pltpu.make_async_copy(weight_hbm, weight_ref, lsem.at[1]),
        pltpu.make_async_copy(cot_hbm, cot_t, lsem.at[2]),
        pltpu.make_async_copy(bas_hbm, bas_g.at[core, x], lsem.at[3]),
        pltpu.make_async_copy(h_src.at[0, pl.ds(keep, 224)], h_keep, lsem.at[4]),
        pltpu.make_async_copy(e_src.at[pl.ds(pl.multiple_of(128 * x, 128), 128)], e_x.at[x], lsem.at[5]),
    ]
    for cp in loads:
        cp.start()

    pl.semaphore_wait(barrier, jnp.where(col == y, 15, 18))

    holder = col == 3

    def last_copies(n):
        return [pltpu.make_async_remote_copy(
            src_ref=src, dst_ref=src_to, send_sem=ssem.at[n + i], recv_sem=rsem.at[R_HL],
            device_id=at_c(k), device_id_type=MESH)
            for i, (src, src_to, k) in enumerate((
                (h_src.at[1, 0:224], h_win.at[1, 0:224], 0),
                (h_src.at[1, 224:448], h_win.at[1, 224:448], 1),
                (h_src.at[1], h_win.at[1], 2)))]

    first_last = used[0]
    used[0] += 3

    @pl.when(holder)
    def _():
        for cp in last_copies(first_last):
            cp.start()
        cp = pltpu.make_async_copy(h_src.at[1], h_win.at[1], lsem.at[7])
        cp.start()
        cp.wait()

    send(h_src.at[0, pl.ds(give, 224)], h_a, R_H, sibling)

    swap = used[0]

    @pl.when(col != y)
    def _():
        copy(act_hbm, act_g.at[y % 2, x], R_TURN, at_yc(col, y))

    @pl.when(col == y)
    def _():
        cp = pltpu.make_async_copy(act_hbm, act_g.at[core, x], lsem.at[6])
        cp.start()
        cp.wait()

    loads[0].wait()
    loads[1].wait()
    ids = jnp.transpose(jnp.broadcast_to(shard_ref[...].astype(F32), (128, 256)))
    lane = lax.broadcasted_iota(jnp.int32, (256, 128), 1).astype(F32)
    weight = jnp.zeros((256, 128), F32)
    for j in range(16):
        weight = weight + jnp.where(ids == lane + float(128 * j), weight_ref[j:j + 1, :], 0.0)
    weight = jnp.sum(weight, axis=1, keepdims=True)

    arrived(R_H, h_a)
    loads[4].wait()
    h_a[...] = h_a[...] + h_keep[...]
    send(h_a, h_b, R_H + 1, partner)
    x_up, x_down, x_far = (x + 1) % 4, (x + 3) % 4, (x + 2) % 4
    loads[2].wait()
    cot[...] = (jnp.transpose(cot_t[...].astype(F32)) * weight).astype(BF16)

    def project(p):
        part = jnp.dot(cot[...], h_win[p], preferred_element_type=F32).astype(BF16)
        for j in range(4):
            p_src[p, j] = part[64 * j:64 * (j + 1)]
        start(R_PY + 4 * p, y, at_y, lambda j: p_src.at[p, j], p_y.at[p, y])
        p_y[p, y] = p_src[p, y]

    @pl.when(zlo == 0)
    def _():
        arrived(R_HL, h_win.at[1, pl.ds(keep, 224)])
        cp = copy(h_win.at[1, pl.ds(keep, 224)], h_win.at[1, pl.ds(keep, 224)], R_HL + 1, sibling)
        arrived(R_HL + 1, h_win.at[1, pl.ds(give, 224)])
        cp.wait_send()

    @pl.when(col == 2)
    def _():
        arrived(R_HL, h_win.at[1])

    project(1)
    arrived(R_H + 1, h_b)
    h_win[0, pl.ds(keep, 224)] = h_a[...] + h_b[...]
    send(h_win.at[0, pl.ds(keep, 224)], h_win.at[0, pl.ds(keep, 224)], R_H + 2, sibling)

    @pl.when(col != y)
    def _():
        arrived(R_TURN, act_g.at[core, x])
    start(R_ACT, x, at_x, lambda j: act_g.at[core, x], act_g.at[core, x])
    send(act_g.at[core, x], act_g.at[core, x], R_ASIB + x, sibling)

    arrived(R_H + 2, h_win.at[0, pl.ds(give, 224)])
    project(0)
    wins = [pltpu.make_async_copy(h_win.at[p], win_out.at[:, PANEL * p:PANEL * (p + 1)], lsem.at[9 + p]) for p in range(2)]
    for cp in wins:
        cp.start()

    @pl.when(holder)
    def _():
        for cp in last_copies(first_last):
            cp.wait_send()

    for p in (1, 0):
        finish(R_PY + 4 * p, y, lambda j: p_y.at[p, j])
        total = add4(p_y[p, 0], p_y[p, 1], p_y[p, 2], p_y[p, 3]).astype(BF16)
        for j in range(2):
            p_x0[2 * p + j] = total[:, 128 * j:128 * (j + 1)]
    start(R_PX, x, at_x, lambda j: p_x0.at[j], p_x.at[x])
    p_x[x] = p_x0[x]
    start(R_EIX, x, at_x, lambda j: e_src.at[pl.ds(pl.multiple_of(128 * j, 128), 128)], e_x.at[x])
    finish(R_PX, x, lambda j: p_x.at[j])

    low, high = pl.ds(0, 1024), pl.ds(1024, 1024)

    def basis(slot, part, recv, j):
        send(bas_g.at[core, slot, part], bas_g.at[core, slot, part], recv, at_x(j))

    loads[3].wait()
    basis(x, low, R_BAS + 0, x_up)
    basis(x, high, R_BAS + 1, x_down)
    p_z0[...] = add4(p_x[0], p_x[1], p_x[2], p_x[3]).astype(BF16)
    start(R_PZ, zh, at_z, lambda j: p_z0, p_z.at[zh])
    p_z[zh] = p_z0[...]
    for d in (1, 3, 2):
        j = (x + d) % 4
        arrived(R_ACT + j, act_g.at[core, j])
        send(act_g.at[core, j], act_g.at[core, j], R_ASIB + j, sibling)

    basis(x, high, R_BAS + 2, x_up)
    basis(x, low, R_BAS + 3, x_down)

    finish(R_PZ, zh, lambda j: p_z.at[j])
    p_s[...] = add4(p_z[0], p_z[1], p_z[2], p_z[3]).astype(BF16)
    first_turn = used[0]
    used[0] += 4

    def turn(k):
        return pltpu.make_async_remote_copy(
            src_ref=p_s, dst_ref=p_g.at[y], send_sem=ssem.at[first_turn + k], recv_sem=rsem.at[R_PG + y],
            device_id=at_yc(col, k), device_id_type=MESH)

    for k in range(4):
        away = (col != y) | (col != k)

        @pl.when(away)
        def _():
            turn(k).start()

        @pl.when(jnp.logical_not(away))
        def _():
            p_g[y] = p_s[...]

    loads[5].wait()
    finish(R_EIX, x, lambda j: e_x.at[j])
    for d in (2, 1, 3):
        j = (col + d) % 4
        half = pl.ds(pl.multiple_of(64 * (j % 2), 64), 64)
        send(e_x.at[:, half], e_c.at[col], R_EIC + col, at_c(j))
    e_c[col] = e_x[:, pl.ds(pl.multiple_of(64 * core, 64), 64)]
    for j in range(4):
        arrived(R_ASIB + j, act_g.at[1 - core, j])
    for j in range(4):
        @pl.when((col != y) | (j != y))
        def _():
            arrived(R_PG + j, p_g.at[j])

    turned_p = jnp.transpose(p_g[...].reshape(256, 128).astype(F32)).astype(BF16)
    pk[0] = turned_p[0:64]
    pk[1] = turned_p[64:128]
    mine = pk[core]
    for q in range(2):
        for j in range(4):
            part = jnp.dot(mine, act_g[q, j], preferred_element_type=F32).astype(BF16)
            for k in range(4):
                r_src[k, q, :, 128 * j:128 * (j + 1)] = part[16 * k:16 * (k + 1)]
    start(R_RY, y, at_y, lambda j: r_src.at[j], r_y.at[y])
    r_y[y] = r_src[y]
    arrived(R_BAS + 0, bas_g.at[core, x_down, low])
    basis(x_down, low, R_BAS + 4, x_up)
    arrived(R_BAS + 1, bas_g.at[core, x_up, high])
    basis(x_up, high, R_BAS + 5, x_down)
    send(bas_g.at[core, x], bas_g.at[core, x], R_SIB + 0, sibling)
    finish(R_RY, y, lambda j: r_y.at[j])
    here = pl.ds(pl.multiple_of(16 * y, 16), 16)
    r_full[zh, :, here] = add4(r_y[0], r_y[1], r_y[2], r_y[3]).astype(BF16)
    start(R_RZ, zh, at_z, lambda j: r_full.at[zh, :, here], r_full.at[zh, :, here])
    start(R_RG + 4 * zh, y, at_y, lambda j: r_full.at[zh, :, here], r_full.at[zh, :, here])
    arrived(R_BAS + 2, bas_g.at[core, x_down, high])
    send(bas_g.at[core, x_down], bas_g.at[core, x_down], R_SIB + 1, sibling)
    arrived(R_BAS + 3, bas_g.at[core, x_up, low])
    send(bas_g.at[core, x_up], bas_g.at[core, x_up], R_SIB + 2, sibling)
    for d in (1, 3, 2):
        z = (zh + d) % 4
        arrived(R_RZ + z, r_full.at[z, :, here])
        start(R_RG + 4 * z, y, at_y, lambda j: r_full.at[z, :, here], r_full.at[z, :, here])
    arrived(R_BAS + 4, bas_g.at[core, x_far, low])
    arrived(R_BAS + 5, bas_g.at[core, x_far, high])
    send(bas_g.at[core, x_far], bas_g.at[core, x_far], R_SIB + 3, sibling)
    for d in (0, 1, 3, 2):
        z = (zh + d) % 4
        for e in (1, 3, 2):
            j = (y + e) % 4
            arrived(R_RG + 4 * z + j, r_full.at[z, :, pl.ds(pl.multiple_of(16 * j, 16), 16)])

    for k in range(4):
        @pl.when((col != y) | (col != k))
        def _():
            turn(k).wait_send()

    for j, slot in ((0, x), (1, x_down), (2, x_up), (3, x_far)):
        arrived(R_SIB + j, bas_g.at[1 - core, slot])
    own = []
    for j in range(4):
        acc = None
        for q in range(2):
            for z in range(4):
                term = jnp.dot(r_full[z, q], bas_g[q, j, 512 * z:512 * (z + 1)], preferred_element_type=F32)
                acc = term if acc is None else acc + term
        own.append(acc)
        t_src[j] = acc.astype(BF16)
    send(t_src, t_in, R_TC, partner)
    finish(R_EIC, col, lambda j: e_c.at[j])
    damped = add4(e_c[0], e_c[1], e_c[2], e_c[3]) + DAMPING
    arrived(R_TC, t_in)
    for j in range(4):
        c_all[j] = ((own[j] + t_in[j].astype(F32)) / damped[j]).astype(BF16)

    z_order = [(zh + d) % 4 for d in (2, 1, 3, 0)]
    for z in z_order:
        for q in range(2):
            acc = None
            for j in range(4):
                term = lax.dot_general(
                    c_all[j], bas_g[q, j, pl.ds(pl.multiple_of(512 * z, 512), 512)], (((1,), (1,)), ((), ())),
                    preferred_element_type=F32)
                acc = term if acc is None else acc + term
            acc = acc.astype(BF16)
            for j in range(4):
                q_src[j, z, q] = acc[16 * j:16 * (j + 1)]
        for d in (2, 1, 3):
            j = (y + d) % 4
            send(q_src.at[j, z], q_y.at[y, z], R_QY + 4 * y + z, at_y(j))
        q_y[y, z] = q_src[y, z]
    for n, z in enumerate(z_order):
        for d in (1, 3, 2):
            j = (y + d) % 4
            arrived(R_QY + 4 * j + z, q_y.at[j, z])
        total = add4(q_y[0, z], q_y[1, z], q_y[2, z], q_y[3, z]).astype(BF16)
        if n < 3:
            q_z0[z] = total
            send(q_z0.at[z], q_z.at[zh], R_QZ + zh, at_z(z))
        else:
            q_z[zh] = total
    finish(R_QZ, zh, lambda j: q_z.at[j])
    piece = add4(q_z[0], q_z[1], q_z[2], q_z[3]).astype(BF16)

    def spot(z):
        return pl.ds(pl.multiple_of(512 * z, 512), 512)

    g_src[...] = piece
    own_ret = pltpu.make_async_copy(g_src.at[core], ret.at[x, core, y, :, spot(zh)], lsem.at[8])
    own_ret.start()
    for d in (2, 1, 3):
        j = (zh + d) % 4
        for k in (core, 1 - core):
            send(g_src.at[k], ret.at[x, core, y, :, spot(zh)], R_GZ + 2 * zh + core, (at_z(j)[0], zlo * 2 + k))
    send(g_src.at[1 - core], ret.at[x, core, y, :, spot(zh)], R_GZ + 2 * zh + core, sibling)
    arrived(R_GZ + 2 * zh + 1 - core, ret.at[x, 1 - core, y, :, spot(zh)])
    for d in (1, 3, 2):
        j = (zh + d) % 4
        for k in range(2):
            arrived(R_GZ + 2 * j + k, ret.at[x, k, y, :, spot(j)])
    own_ret.wait()

    whole, part_a, part_b = 0, 1, 2
    y_up, y_down, y_far = (y + 1) % 4, (y + 3) % 4, (y + 2) % 4
    x_ring = (x, x_up, x_down, x_far, at_x)
    y_ring = (y, y_up, y_down, y_far, at_y)

    def give_both(ring, base, block):
        me, up, down, far, place = ring
        send(block(me, whole), block(me, whole), base, place(up))
        send(block(me, whole), block(me, whole), base + 1, place(down))

    def pass_on(ring, base, block, side):
        me, up, down, far, place = ring
        if side == 0:
            arrived(base, block(down, whole))
            send(block(down, part_a), block(down, part_a), base + 2, place(up))
        else:
            arrived(base + 1, block(up, whole))
            send(block(up, part_b), block(up, part_b), base + 3, place(down))

    def take_far(ring, base, block):
        me, up, down, far, place = ring
        arrived(base + 2, block(far, part_a))
        arrived(base + 3, block(far, part_b))

    def gx(j, part):
        return ret.at[j, :, y, :, (slice(0, 2048), slice(0, 1024), slice(1024, 2048))[part]]

    def gy(j, part):
        return ret.at[x, :, j, :, (slice(0, 2048), slice(0, 1024), slice(1024, 2048))[part]]

    def fx(k):
        return lambda j, part: ret.at[j, :, k, :, (slice(0, 1024), slice(0, 512), slice(512, 1024))[part]]

    def fy(k):
        return lambda j, part: ret.at[k, :, j, :, (slice(1024, 2048), slice(1024, 1536), slice(1536, 2048))[part]]

    give_both(x_ring, R_GX, gx)
    give_both(y_ring, R_GY, gy)
    near = ((0, y_down, x_down), (1, y_up, x_up))
    for side, ky, kx in near:
        pass_on(y_ring, R_GY, gy, side)
        give_both(x_ring, R_FX + 4 * side, fx(ky))
        pass_on(x_ring, R_GX, gx, side)
        give_both(y_ring, R_FY + 4 * side, fy(kx))
    take_far(y_ring, R_GY, gy)
    give_both(x_ring, R_FX + 8, fx(y_far))
    take_far(x_ring, R_GX, gx)
    give_both(y_ring, R_FY + 8, fy(x_far))
    cols = ((0, y_down, x_down), (1, y_up, x_up), (2, y_far, x_far))
    for n, ky, kx in cols:
        for side in range(2):
            pass_on(x_ring, R_FX + 4 * n, fx(ky), side)
            pass_on(y_ring, R_FY + 4 * n, fy(kx), side)
    for n, ky, kx in cols:
        take_far(x_ring, R_FX + 4 * n, fx(ky))
        take_far(y_ring, R_FY + 4 * n, fy(kx))
    for cp in wins:
        cp.wait()
    assert used[0] <= N_SEND
    for cp in sends:
        cp.wait_send()

    @pl.when(col != y)
    def _():
        pltpu.make_async_remote_copy(
            src_ref=act_hbm, dst_ref=act_g.at[y % 2, x], send_sem=ssem.at[swap], recv_sem=rsem.at[R_TURN],
            device_id=at_yc(col, y), device_id_type=MESH).wait_send()


def per_device(cotangent, activations, shard_of_token, shard_weight, hidden_basis, input_basis, eigenvalues, panel_order):
    vmem = pl.BlockSpec(memory_space=pltpu.VMEM)
    hbm = pl.BlockSpec(memory_space=pltpu.HBM)

    def buf(*shape):
        return pltpu.VMEM(shape, BF16)

    h_src, e_src = pl.pallas_call(
        pick,
        out_shape=[jax.ShapeDtypeStruct((2, 448, 256), BF16), jax.ShapeDtypeStruct((512, 128), BF16)],
        in_specs=[hbm, hbm, hbm],
        out_specs=[vmem, vmem],
        scratch_shapes=[pltpu.SMEM((2,), jnp.int32), pltpu.SemaphoreType.DMA((5,))],
        compiler_params=pltpu.CompilerParams(vmem_limit_bytes=40 * 1024 * 1024),
        name="pick",
    )(*[pltpu.with_memory_space_constraint(a, pltpu.HBM) for a in (panel_order, hidden_basis, eigenvalues)])

    ret, win = pl.pallas_call(
        kernel,
        out_shape=[jax.ShapeDtypeStruct((4, 2, 4, 16, 2048), BF16), jax.ShapeDtypeStruct((448, 512), BF16)],
        in_specs=[hbm] * 7,
        out_specs=[hbm, hbm],
        scratch_shapes=[
            buf(448, 256), buf(256, 448), pltpu.VMEM((1, 256), jnp.int32), pltpu.VMEM((16, 128), F32),
            buf(2, 4, 256, 128), buf(2, 4, 2048, 128),
            buf(4, 128, 128), buf(4, 4, 64, 128),
            buf(224, 256), buf(224, 256), buf(224, 256), buf(2, 448, 256),
            buf(2, 4, 64, 256), buf(2, 4, 64, 256), buf(4, 64, 128), buf(4, 64, 128), buf(64, 128), buf(4, 64, 128),
            buf(64, 128), buf(4, 64, 128),
            buf(2, 64, 256), buf(4, 2, 16, 512), buf(4, 2, 16, 512), buf(4, 2, 64, 512),
            buf(4, 64, 128), buf(4, 64, 128), buf(4, 64, 128),
            buf(4, 4, 2, 16, 512), buf(4, 4, 2, 16, 512), buf(4, 2, 16, 512), buf(4, 2, 16, 512), buf(2, 16, 512),
            pltpu.SemaphoreType.DMA((N_SEND,)),
            pltpu.SemaphoreType.DMA((N_RECV,)),
            pltpu.SemaphoreType.DMA((11,)),
        ],
        compiler_params=pltpu.CompilerParams(
            collective_id=0, has_side_effects=True, vmem_limit_bytes=50 * 1024 * 1024),
        cost_estimate=pl.CostEstimate(flops=3_000_000_000, bytes_accessed=12_000_000, transcendentals=0),
        name="influence",
    )(*[
        pltpu.with_memory_space_constraint(a, pltpu.HBM)
        for a in (cotangent.T, activations, shard_of_token.reshape(1, 256), shard_weight.reshape(16, 128), input_basis)
    ] + [h_src, e_src])

    return jnp.dot(win, ret.reshape(512, 2048), preferred_element_type=F32).astype(BF16)


def solution(mesh):
    placed = (
        P("col", "row"),
        P("col", "row"),
        P("col"),
        P(),
        P("row", "col"),
        P("col", "row"),
        P("col", "row"),
        P(),
    )
    return jax.shard_map(
        per_device, mesh=mesh, in_specs=placed, out_specs=P("row", "col"), check_vma=False
    )
```

```python
import jax
import jax.numpy as jnp
from jax import lax
from jax.experimental import pallas as pl
from jax.experimental.pallas import tpu as pltpu
from jax.sharding import PartitionSpec as P

PANEL = 256
LAST = 111
PER_COL = 28
DAMPING = 0.01
MESH = pl.DeviceIdType.MESH
F32 = jnp.float32
BF16 = jnp.bfloat16

(R_TURN, R_ACT, R_ASIB, R_BAS, R_SIB, R_EIX, R_EIC, R_H, R_HL, R_PY, R_PX, R_PZ, R_PG, R_RY, R_RZ, R_RG, R_TC, R_QY, R_QZ,
 R_GZ, R_GX, R_GY, R_FX, R_FY) = (
    0, 1, 5, 9, 15, 19, 23, 27, 30, 32, 40, 44, 48, 52, 56, 60, 76, 77, 93, 97, 105, 109, 113, 125)
N_RECV = 137
N_SEND = 160


def pick(order_hbm, hid_hbm, eig_hbm, h_src, e_src, order, sems):
    col = lax.axis_index("col")
    cp = pltpu.make_async_copy(order_hbm, order, sems.at[0])
    cp.start()
    cp.wait()
    other = order[0] + order[1] - LAST
    place = pl.multiple_of((other - col * PER_COL) * PANEL, PANEL)
    mine = (other >= col * PER_COL) & (other < (col + 1) * PER_COL)
    end = (PER_COL - 1) * PANEL

    def fetch(have, at, k):
        h_part = h_src.at[k]
        e_part = e_src.at[PANEL * k:PANEL * (k + 1)]

        def copies():
            return (pltpu.make_async_copy(hid_hbm.at[:, pl.ds(at, PANEL)], h_part, sems.at[1 + 2 * k]),
                    pltpu.make_async_copy(eig_hbm.at[pl.ds(at, PANEL)], e_part, sems.at[2 + 2 * k]))

        @pl.when(have)
        def _():
            for cp in copies():
                cp.start()

        @pl.when(jnp.logical_not(have))
        def _():
            h_part[...] = jnp.zeros(h_part.shape, BF16)
            e_part[...] = jnp.zeros(e_part.shape, BF16)

        def settle():
            @pl.when(have)
            def _():
                for cp in copies():
                    cp.wait()
        return settle

    settle = [fetch(mine, place, 0), fetch(col == 3, end, 1)]
    for wait in settle:
        wait()


def add4(a, b, c, d):
    return (a.astype(F32) + b.astype(F32)) + (c.astype(F32) + d.astype(F32))


def kernel(
    cot_hbm, act_hbm, shard_hbm, weight_hbm, bas_hbm, h_src, e_src, ret, win_out,
    cot_t, cot, shard_ref, weight_ref, act_g, bas_g,
    e_x, e_c,
    h_keep, h_a, h_b, h_win,
    p_src, p_y, p_x0, p_x, p_z0, p_z, p_s, p_g,
    pk, r_src, r_y, r_full,
    t_src, t_in, c_all,
    q_src, q_y, q_z0, q_z, g_src,
    ssem, rsem, lsem,
):
    row = lax.axis_index("row")
    col = lax.axis_index("col")
    x = row % 4
    zh = (row // 4) % 4
    y = row // 16
    core = col % 2
    zlo = col // 2

    def at_x(j):
        return (y * 16 + zh * 4 + j, col)

    def at_y(j):
        return (j * 16 + zh * 4 + x, col)

    def at_z(j):
        return (y * 16 + j * 4 + x, col)

    def at_c(j):
        return (row, j)

    def at_yc(j, k):
        return (j * 16 + zh * 4 + x, k)

    sibling = at_c(zlo * 2 + 1 - core)
    partner = at_c((col + 2) % 4)

    sends = []
    used = [0]

    def copy(src, dst, recv, device):
        cp = pltpu.make_async_remote_copy(
            src_ref=src, dst_ref=dst, send_sem=ssem.at[used[0]], recv_sem=rsem.at[recv],
            device_id=device, device_id_type=MESH)
        used[0] += 1
        cp.start()
        return cp

    def send(src, dst, recv, device):
        sends.append(copy(src, dst, recv, device))

    def arrived(recv, dst):
        pltpu.make_async_remote_copy(
            src_ref=dst, dst_ref=dst, send_sem=ssem.at[0], recv_sem=rsem.at[recv],
            device_id=sibling, device_id_type=MESH).wait_recv()

    def start(base, me, place, src_of, dst):
        for d in (2, 1, 3):
            j = (me + d) % 4
            send(src_of(j), dst, base + me, place(j))

    def finish(base, me, dst_of):
        for d in (1, 3, 2):
            j = (me + d) % 4
            arrived(base + j, dst_of(j))

    barrier = pltpu.get_barrier_semaphore()
    for d in (1, 2, 3):
        pl.semaphore_signal(barrier, inc=1, device_id=at_c((col + d) % 4), device_id_type=MESH)
    for me, place in ((x, at_x), (y, at_y), (zh, at_z)):
        for d in (2, 1, 3):
            pl.semaphore_signal(barrier, inc=1, device_id=place((me + d) % 4), device_id_type=MESH)
    for d in (2, 1, 3):
        pl.semaphore_signal(
            barrier, inc=1, device_id=(at_z((zh + d) % 4)[0], zlo * 2 + 1 - core), device_id_type=MESH)


    @pl.when(col != y)
    def _():
        for d in (2, 1, 3):
            pl.semaphore_signal(barrier, inc=1, device_id=at_yc((y + d) % 4, y), device_id_type=MESH)

    keep = pl.multiple_of(core * 224, 224)
    give = pl.multiple_of((1 - core) * 224, 224)
    loads = [
        pltpu.make_async_copy(shard_hbm, shard_ref, lsem.at[0]),
        pltpu.make_async_copy(weight_hbm, weight_ref, lsem.at[1]),
        pltpu.make_async_copy(cot_hbm, cot_t, lsem.at[2]),
        pltpu.make_async_copy(bas_hbm, bas_g.at[core, x], lsem.at[3]),
        pltpu.make_async_copy(h_src.at[0, pl.ds(keep, 224)], h_keep, lsem.at[4]),
        pltpu.make_async_copy(e_src.at[pl.ds(pl.multiple_of(128 * x, 128), 128)], e_x.at[x], lsem.at[5]),
    ]
    for cp in loads:
        cp.start()

    pl.semaphore_wait(barrier, jnp.where(col == y, 15, 18))

    holder = col == 3

    def last_copies(n):
        return [pltpu.make_async_remote_copy(
            src_ref=src, dst_ref=src_to, send_sem=ssem.at[n + i], recv_sem=rsem.at[R_HL],
            device_id=at_c(k), device_id_type=MESH)
            for i, (src, src_to, k) in enumerate((
                (h_src.at[1, 0:224], h_win.at[1, 0:224], 0),
                (h_src.at[1, 224:448], h_win.at[1, 224:448], 1),
                (h_src.at[1], h_win.at[1], 2)))]

    first_last = used[0]
    used[0] += 3

    @pl.when(holder)
    def _():
        for cp in last_copies(first_last):
            cp.start()
        cp = pltpu.make_async_copy(h_src.at[1], h_win.at[1], lsem.at[7])
        cp.start()
        cp.wait()

    send(h_src.at[0, pl.ds(give, 224)], h_a, R_H, sibling)

    swap = used[0]

    @pl.when(col != y)
    def _():
        copy(act_hbm, act_g.at[y % 2, x], R_TURN, at_yc(col, y))

    @pl.when(col == y)
    def _():
        cp = pltpu.make_async_copy(act_hbm, act_g.at[core, x], lsem.at[6])
        cp.start()
        cp.wait()

    loads[0].wait()
    loads[1].wait()
    ids = jnp.transpose(jnp.broadcast_to(shard_ref[...].astype(F32), (128, 256)))
    lane = lax.broadcasted_iota(jnp.int32, (256, 128), 1).astype(F32)
    weight = jnp.zeros((256, 128), F32)
    for j in range(16):
        weight = weight + jnp.where(ids == lane + float(128 * j), weight_ref[j:j + 1, :], 0.0)
    weight = jnp.sum(weight, axis=1, keepdims=True)

    arrived(R_H, h_a)
    loads[4].wait()
    h_a[...] = h_a[...] + h_keep[...]
    send(h_a, h_b, R_H + 1, partner)
    x_up, x_down, x_far = (x + 1) % 4, (x + 3) % 4, (x + 2) % 4
    loads[2].wait()
    cot[...] = (jnp.transpose(cot_t[...].astype(F32)) * weight).astype(BF16)

    def project(p):
        part = jnp.dot(cot[...], h_win[p], preferred_element_type=F32).astype(BF16)
        for j in range(4):
            p_src[p, j] = part[64 * j:64 * (j + 1)]
        start(R_PY + 4 * p, y, at_y, lambda j: p_src.at[p, j], p_y.at[p, y])
        p_y[p, y] = p_src[p, y]

    @pl.when(zlo == 0)
    def _():
        arrived(R_HL, h_win.at[1, pl.ds(keep, 224)])
        cp = copy(h_win.at[1, pl.ds(keep, 224)], h_win.at[1, pl.ds(keep, 224)], R_HL + 1, sibling)
        arrived(R_HL + 1, h_win.at[1, pl.ds(give, 224)])
        cp.wait_send()

    @pl.when(col == 2)
    def _():
        arrived(R_HL, h_win.at[1])

    project(1)
    arrived(R_H + 1, h_b)
    h_win[0, pl.ds(keep, 224)] = h_a[...] + h_b[...]
    send(h_win.at[0, pl.ds(keep, 224)], h_win.at[0, pl.ds(keep, 224)], R_H + 2, sibling)

    @pl.when(col != y)
    def _():
        arrived(R_TURN, act_g.at[core, x])
    start(R_ACT, x, at_x, lambda j: act_g.at[core, x], act_g.at[core, x])
    send(act_g.at[core, x], act_g.at[core, x], R_ASIB + x, sibling)

    arrived(R_H + 2, h_win.at[0, pl.ds(give, 224)])
    project(0)
    wins = [pltpu.make_async_copy(h_win.at[p], win_out.at[:, PANEL * p:PANEL * (p + 1)], lsem.at[9 + p]) for p in range(2)]
    for cp in wins:
        cp.start()

    @pl.when(holder)
    def _():
        for cp in last_copies(first_last):
            cp.wait_send()

    for p in (1, 0):
        finish(R_PY + 4 * p, y, lambda j: p_y.at[p, j])
        total = add4(p_y[p, 0], p_y[p, 1], p_y[p, 2], p_y[p, 3]).astype(BF16)
        for j in range(2):
            p_x0[2 * p + j] = total[:, 128 * j:128 * (j + 1)]
    start(R_PX, x, at_x, lambda j: p_x0.at[j], p_x.at[x])
    p_x[x] = p_x0[x]
    start(R_EIX, x, at_x, lambda j: e_src.at[pl.ds(pl.multiple_of(128 * j, 128), 128)], e_x.at[x])
    finish(R_PX, x, lambda j: p_x.at[j])

    low, high = pl.ds(0, 1024), pl.ds(1024, 1024)

    def basis(slot, part, recv, j):
        send(bas_g.at[core, slot, part], bas_g.at[core, slot, part], recv, at_x(j))

    loads[3].wait()
    basis(x, low, R_BAS + 0, x_up)
    basis(x, high, R_BAS + 1, x_down)
    send(bas_g.at[core, x], bas_g.at[core, x], R_SIB + 0, sibling)
    p_z0[...] = add4(p_x[0], p_x[1], p_x[2], p_x[3]).astype(BF16)
    start(R_PZ, zh, at_z, lambda j: p_z0, p_z.at[zh])
    p_z[zh] = p_z0[...]
    for d in (1, 3, 2):
        j = (x + d) % 4
        arrived(R_ACT + j, act_g.at[core, j])
        send(act_g.at[core, j], act_g.at[core, j], R_ASIB + j, sibling)

    basis(x, high, R_BAS + 2, x_up)
    basis(x, low, R_BAS + 3, x_down)

    finish(R_PZ, zh, lambda j: p_z.at[j])
    p_s[...] = add4(p_z[0], p_z[1], p_z[2], p_z[3]).astype(BF16)
    first_turn = used[0]
    used[0] += 4

    def turn(k):
        return pltpu.make_async_remote_copy(
            src_ref=p_s, dst_ref=p_g.at[y], send_sem=ssem.at[first_turn + k], recv_sem=rsem.at[R_PG + y],
            device_id=at_yc(col, k), device_id_type=MESH)

    for k in range(4):
        away = (col != y) | (col != k)

        @pl.when(away)
        def _():
            turn(k).start()

        @pl.when(jnp.logical_not(away))
        def _():
            p_g[y] = p_s[...]

    arrived(R_BAS + 0, bas_g.at[core, x_down, low])
    basis(x_down, low, R_BAS + 4, x_up)
    arrived(R_BAS + 1, bas_g.at[core, x_up, high])
    basis(x_up, high, R_BAS + 5, x_down)
    loads[5].wait()
    finish(R_EIX, x, lambda j: e_x.at[j])
    for d in (2, 1, 3):
        j = (col + d) % 4
        half = pl.ds(pl.multiple_of(64 * (j % 2), 64), 64)
        send(e_x.at[:, half], e_c.at[col], R_EIC + col, at_c(j))
    e_c[col] = e_x[:, pl.ds(pl.multiple_of(64 * core, 64), 64)]
    for j in range(4):
        arrived(R_ASIB + j, act_g.at[1 - core, j])
    for j in range(4):
        @pl.when((col != y) | (j != y))
        def _():
            arrived(R_PG + j, p_g.at[j])

    turned_p = jnp.transpose(p_g[...].reshape(256, 128).astype(F32)).astype(BF16)
    pk[0] = turned_p[0:64]
    pk[1] = turned_p[64:128]
    mine = pk[core]
    for q in range(2):
        for j in range(4):
            part = jnp.dot(mine, act_g[q, j], preferred_element_type=F32).astype(BF16)
            for k in range(4):
                r_src[k, q, :, 128 * j:128 * (j + 1)] = part[16 * k:16 * (k + 1)]
    start(R_RY, y, at_y, lambda j: r_src.at[j], r_y.at[y])
    r_y[y] = r_src[y]
    finish(R_RY, y, lambda j: r_y.at[j])
    here = pl.ds(pl.multiple_of(16 * y, 16), 16)
    r_full[zh, :, here] = add4(r_y[0], r_y[1], r_y[2], r_y[3]).astype(BF16)
    start(R_RZ, zh, at_z, lambda j: r_full.at[zh, :, here], r_full.at[zh, :, here])
    start(R_RG + 4 * zh, y, at_y, lambda j: r_full.at[zh, :, here], r_full.at[zh, :, here])
    arrived(R_BAS + 2, bas_g.at[core, x_down, high])
    send(bas_g.at[core, x_down], bas_g.at[core, x_down], R_SIB + 1, sibling)
    arrived(R_BAS + 3, bas_g.at[core, x_up, low])
    send(bas_g.at[core, x_up], bas_g.at[core, x_up], R_SIB + 2, sibling)
    for d in (1, 3, 2):
        z = (zh + d) % 4
        arrived(R_RZ + z, r_full.at[z, :, here])
        start(R_RG + 4 * z, y, at_y, lambda j: r_full.at[z, :, here], r_full.at[z, :, here])
    arrived(R_BAS + 4, bas_g.at[core, x_far, low])
    arrived(R_BAS + 5, bas_g.at[core, x_far, high])
    send(bas_g.at[core, x_far], bas_g.at[core, x_far], R_SIB + 3, sibling)
    for d in (0, 1, 3, 2):
        z = (zh + d) % 4
        for e in (1, 3, 2):
            j = (y + e) % 4
            arrived(R_RG + 4 * z + j, r_full.at[z, :, pl.ds(pl.multiple_of(16 * j, 16), 16)])

    for k in range(4):
        @pl.when((col != y) | (col != k))
        def _():
            turn(k).wait_send()

    for j, slot in ((0, x), (1, x_down), (2, x_up), (3, x_far)):
        arrived(R_SIB + j, bas_g.at[1 - core, slot])
    own = []
    for j in range(4):
        acc = None
        for q in range(2):
            for z in range(4):
                term = jnp.dot(r_full[z, q], bas_g[q, j, 512 * z:512 * (z + 1)], preferred_element_type=F32)
                acc = term if acc is None else acc + term
        own.append(acc)
        t_src[j] = acc.astype(BF16)
    send(t_src, t_in, R_TC, partner)
    finish(R_EIC, col, lambda j: e_c.at[j])
    damped = add4(e_c[0], e_c[1], e_c[2], e_c[3]) + DAMPING
    arrived(R_TC, t_in)
    for j in range(4):
        c_all[j] = ((own[j] + t_in[j].astype(F32)) / damped[j]).astype(BF16)

    z_order = [(zh + d) % 4 for d in (2, 1, 3, 0)]
    for z in z_order:
        for q in range(2):
            acc = None
            for j in range(4):
                term = lax.dot_general(
                    c_all[j], bas_g[q, j, pl.ds(pl.multiple_of(512 * z, 512), 512)], (((1,), (1,)), ((), ())),
                    preferred_element_type=F32)
                acc = term if acc is None else acc + term
            acc = acc.astype(BF16)
            for j in range(4):
                q_src[j, z, q] = acc[16 * j:16 * (j + 1)]
        for d in (2, 1, 3):
            j = (y + d) % 4
            send(q_src.at[j, z], q_y.at[y, z], R_QY + 4 * y + z, at_y(j))
        q_y[y, z] = q_src[y, z]
    for n, z in enumerate(z_order):
        for d in (1, 3, 2):
            j = (y + d) % 4
            arrived(R_QY + 4 * j + z, q_y.at[j, z])
        total = add4(q_y[0, z], q_y[1, z], q_y[2, z], q_y[3, z]).astype(BF16)
        if n < 3:
            q_z0[z] = total
            send(q_z0.at[z], q_z.at[zh], R_QZ + zh, at_z(z))
        else:
            q_z[zh] = total
    finish(R_QZ, zh, lambda j: q_z.at[j])
    piece = add4(q_z[0], q_z[1], q_z[2], q_z[3]).astype(BF16)

    def spot(z):
        return pl.ds(pl.multiple_of(512 * z, 512), 512)

    g_src[...] = piece
    own_ret = pltpu.make_async_copy(g_src.at[core], ret.at[x, core, y, :, spot(zh)], lsem.at[8])
    own_ret.start()
    for d in (2, 1, 3):
        j = (zh + d) % 4
        for k in (core, 1 - core):
            send(g_src.at[k], ret.at[x, core, y, :, spot(zh)], R_GZ + 2 * zh + core, (at_z(j)[0], zlo * 2 + k))
    send(g_src.at[1 - core], ret.at[x, core, y, :, spot(zh)], R_GZ + 2 * zh + core, sibling)
    arrived(R_GZ + 2 * zh + 1 - core, ret.at[x, 1 - core, y, :, spot(zh)])
    for d in (1, 3, 2):
        j = (zh + d) % 4
        for k in range(2):
            arrived(R_GZ + 2 * j + k, ret.at[x, k, y, :, spot(j)])
    own_ret.wait()

    whole, part_a, part_b = 0, 1, 2
    y_up, y_down, y_far = (y + 1) % 4, (y + 3) % 4, (y + 2) % 4
    x_ring = (x, x_up, x_down, x_far, at_x)
    y_ring = (y, y_up, y_down, y_far, at_y)

    def give_both(ring, base, block):
        me, up, down, far, place = ring
        send(block(me, whole), block(me, whole), base, place(up))
        send(block(me, whole), block(me, whole), base + 1, place(down))

    def pass_on(ring, base, block, side):
        me, up, down, far, place = ring
        if side == 0:
            arrived(base, block(down, whole))
            send(block(down, part_a), block(down, part_a), base + 2, place(up))
        else:
            arrived(base + 1, block(up, whole))
            send(block(up, part_b), block(up, part_b), base + 3, place(down))

    def take_far(ring, base, block):
        me, up, down, far, place = ring
        arrived(base + 2, block(far, part_a))
        arrived(base + 3, block(far, part_b))

    def gx(j, part):
        return ret.at[j, :, y, :, (slice(0, 2048), slice(0, 1024), slice(1024, 2048))[part]]

    def gy(j, part):
        return ret.at[x, :, j, :, (slice(0, 2048), slice(0, 1024), slice(1024, 2048))[part]]

    def fx(k):
        return lambda j, part: ret.at[j, :, k, :, (slice(0, 1024), slice(0, 512), slice(512, 1024))[part]]

    def fy(k):
        return lambda j, part: ret.at[k, :, j, :, (slice(1024, 2048), slice(1024, 1536), slice(1536, 2048))[part]]

    give_both(x_ring, R_GX, gx)
    give_both(y_ring, R_GY, gy)
    near = ((0, y_down, x_down), (1, y_up, x_up))
    for side, ky, kx in near:
        pass_on(y_ring, R_GY, gy, side)
        give_both(x_ring, R_FX + 4 * side, fx(ky))
        pass_on(x_ring, R_GX, gx, side)
        give_both(y_ring, R_FY + 4 * side, fy(kx))
    take_far(y_ring, R_GY, gy)
    give_both(x_ring, R_FX + 8, fx(y_far))
    take_far(x_ring, R_GX, gx)
    give_both(y_ring, R_FY + 8, fy(x_far))
    cols = ((0, y_down, x_down), (1, y_up, x_up), (2, y_far, x_far))
    for n, ky, kx in cols:
        for side in range(2):
            pass_on(x_ring, R_FX + 4 * n, fx(ky), side)
            pass_on(y_ring, R_FY + 4 * n, fy(kx), side)
    for n, ky, kx in cols:
        take_far(x_ring, R_FX + 4 * n, fx(ky))
        take_far(y_ring, R_FY + 4 * n, fy(kx))
    for cp in wins:
        cp.wait()
    assert used[0] <= N_SEND
    for cp in sends:
        cp.wait_send()

    @pl.when(col != y)
    def _():
        pltpu.make_async_remote_copy(
            src_ref=act_hbm, dst_ref=act_g.at[y % 2, x], send_sem=ssem.at[swap], recv_sem=rsem.at[R_TURN],
            device_id=at_yc(col, y), device_id_type=MESH).wait_send()


def per_device(cotangent, activations, shard_of_token, shard_weight, hidden_basis, input_basis, eigenvalues, panel_order):
    vmem = pl.BlockSpec(memory_space=pltpu.VMEM)
    hbm = pl.BlockSpec(memory_space=pltpu.HBM)

    def buf(*shape):
        return pltpu.VMEM(shape, BF16)

    h_src, e_src = pl.pallas_call(
        pick,
        out_shape=[jax.ShapeDtypeStruct((2, 448, 256), BF16), jax.ShapeDtypeStruct((512, 128), BF16)],
        in_specs=[hbm, hbm, hbm],
        out_specs=[vmem, vmem],
        scratch_shapes=[pltpu.SMEM((2,), jnp.int32), pltpu.SemaphoreType.DMA((5,))],
        compiler_params=pltpu.CompilerParams(vmem_limit_bytes=40 * 1024 * 1024),
        name="pick",
    )(*[pltpu.with_memory_space_constraint(a, pltpu.HBM) for a in (panel_order, hidden_basis, eigenvalues)])

    ret, win = pl.pallas_call(
        kernel,
        out_shape=[jax.ShapeDtypeStruct((4, 2, 4, 16, 2048), BF16), jax.ShapeDtypeStruct((448, 512), BF16)],
        in_specs=[hbm] * 7,
        out_specs=[hbm, hbm],
        scratch_shapes=[
            buf(448, 256), buf(256, 448), pltpu.VMEM((1, 256), jnp.int32), pltpu.VMEM((16, 128), F32),
            buf(2, 4, 256, 128), buf(2, 4, 2048, 128),
            buf(4, 128, 128), buf(4, 4, 64, 128),
            buf(224, 256), buf(224, 256), buf(224, 256), buf(2, 448, 256),
            buf(2, 4, 64, 256), buf(2, 4, 64, 256), buf(4, 64, 128), buf(4, 64, 128), buf(64, 128), buf(4, 64, 128),
            buf(64, 128), buf(4, 64, 128),
            buf(2, 64, 256), buf(4, 2, 16, 512), buf(4, 2, 16, 512), buf(4, 2, 64, 512),
            buf(4, 64, 128), buf(4, 64, 128), buf(4, 64, 128),
            buf(4, 4, 2, 16, 512), buf(4, 4, 2, 16, 512), buf(4, 2, 16, 512), buf(4, 2, 16, 512), buf(2, 16, 512),
            pltpu.SemaphoreType.DMA((N_SEND,)),
            pltpu.SemaphoreType.DMA((N_RECV,)),
            pltpu.SemaphoreType.DMA((11,)),
        ],
        compiler_params=pltpu.CompilerParams(
            collective_id=0, has_side_effects=True, vmem_limit_bytes=50 * 1024 * 1024),
        cost_estimate=pl.CostEstimate(flops=3_000_000_000, bytes_accessed=12_000_000, transcendentals=0),
        name="influence",
    )(*[
        pltpu.with_memory_space_constraint(a, pltpu.HBM)
        for a in (cotangent.T, activations, shard_of_token.reshape(1, 256), shard_weight.reshape(16, 128), input_basis)
    ] + [h_src, e_src])

    return jnp.dot(win, ret.reshape(512, 2048), preferred_element_type=F32).astype(BF16)


def solution(mesh):
    placed = (
        P("col", "row"),
        P("col", "row"),
        P("col"),
        P(),
        P("row", "col"),
        P("col", "row"),
        P("col", "row"),
        P(),
    )
    return jax.shard_map(
        per_device, mesh=mesh, in_specs=placed, out_specs=P("row", "col"), check_vma=False
    )
```
